32 devices in a mesh: dp: 16 (over z, y, core), tensor: 2 (over x).
Axes of the slice: x: 2, y: 2, z: 4, core: 2. Of those that a mesh axis runs over, the one named last changes fastest.
Arguments:
- tokens: bfloat16 [32, 256, 768], P('dp'), may hold values from -6 to 6
- segment_ids: int32 [32, 256], P('dp'), may hold values from 0 to 5, never falling along the last dimension, each value on 1 to 64 neighbouring positions
- w_qkv: bfloat16 [768, 3, 768], P(None, None, 'tensor'), may hold values from -0.21875 to 0.21875
- qv_bias: bfloat16 [2, 768], P(None, 'tensor'), may hold values from -3 to 3
- w_out: bfloat16 [768, 768], P(None, 'tensor'), may hold values from -0.625 to 0.625
- out_bias: bfloat16 [768], replicated, may hold values from -2 to 2
- w_in: bfloat16 [768, 3072], P(None, 'tensor'), may hold values from -0.21875 to 0.21875
- hidden_bias: bfloat16 [3072], P('tensor'), may hold values from -3 to 3
- w_down: bfloat16 [768, 3072], P(None, 'tensor'), may hold values from -0.15625 to 0.15625
- mlp_bias: bfloat16 [768], replicated, may hold values from -2 to 2
- ln_gain: bfloat16 [2, 768], replicated, may hold values from 0.5 to 1.5
- ln_bias: bfloat16 [2, 768], replicated, may hold values from -2 to 2
- cotangent: bfloat16 [32, 256, 768], P('dp'), may hold values from -6 to 6
Outputs:
- block_out: bfloat16 [32, 256, 768], P('dp')
- grad_tokens: bfloat16 [32, 256, 768], P('dp')
- grad_w_qkv: float32 [768, 3, 768], P('dp', None, 'tensor')
- grad_qv_bias: float32 [2, 768], P(None, 'tensor')
- grad_w_out: float32 [768, 768], P('dp', 'tensor')
- grad_out_bias: float32 [768], replicated
- grad_w_in: float32 [768, 3072], P('dp', 'tensor')
- grad_hidden_bias: float32 [3072], P('tensor')
- grad_w_down: float32 [768, 3072], P('dp', 'tensor')
- grad_mlp_bias: float32 [768], replicated
- grad_ln_gain: float32 [2, 768], replicated
- grad_ln_bias: float32 [2, 768], replicated
The draws below stay inside these ranges and needn't reach their ends.
Inputs may be any that keep to these rules, and one draw needn't show every extreme that they name: `segment_ids`: along each packed sequence the ids never fall; each image holds 1 to 64 consecutive tokens, and in each sequence some image holds exactly 64.
All inputs are finite; a program needn't handle non-finite values.
Results may differ from the reference program's by a relative error of at most 0.017.
Values may be sent and summed in bfloat16 or wider, within the bound.
A program may use at most 128 MiB of HBM per device.

```python
import math
import jax
import jax.numpy as jnp
import numpy as np
from jax import lax

D = 768
HEADS = 12
HEAD_DIM = 64
FF = 3072
LEN = 256
SEQS = 32
N_TENSOR = 2


def spiked(values, own_key, source, target, shards_of, factor):
    owner, partner = [(jnp.arange(values.shape[axis_at]) // (values.shape[axis_at] // shards_of)).reshape([-1 if axis == axis_at else 1 for axis in range(values.ndim)]) for axis_at in (source, target)]
    chosen = jax.random.permutation(own_key, shards_of)[partner]
    strong = (owner == chosen) | (owner == (partner + shards_of // 2) % shards_of)
    return jnp.where(strong, factor * values, values)


def levels(key, extent, split, least, top_value):
    def one(dim, parts):
        draws = jax.random.uniform(jax.random.fold_in(jax.random.fold_in(key, 6), dim), (parts,), jnp.float32, least / len(split), top_value / len(split))
        return jnp.repeat(jnp.exp(draws), extent[dim] // parts).reshape((-1,) + (1,) * (len(extent) - dim - 1))

    loudness = one(*split[0])
    for cut in split[1:]:
        loudness = loudness * one(*cut)
    return loudness


def profile(amount, total, most, skew):
    loads = [(1 << 20) // math.isqrt(grade ** skew) + 1 for grade in range(2, amount + 1)]
    rest, counts = total - most - (amount - 1), [1] * (amount - 1)
    while rest > 0:
        free = [i for i in range(amount - 1) if counts[i] < most]
        whole, budget = sum([loads[i] for i in free]), rest
        for i in free:
            more = min(most - counts[i], max(1, budget * loads[i] // whole), rest)
            counts[i] = counts[i] + more
            rest = rest - more
    return np.array([most] + counts)


def uneven(rng, number_of, total, reach, skew):
    if number_of == 2:
        one = jax.random.randint(rng, (), max(1, total - reach), min(reach, total - 1) + 1)
        return jnp.stack([one, total - one])
    lengths = jnp.asarray(profile(number_of, total, reach, skew), jnp.int32)
    couples = (number_of - 1) // 2
    donor, taker = lengths[1:1 + 2 * couples:2], lengths[2:2 + 2 * couples:2]
    room = jnp.minimum(donor - 1, reach - taker)
    shifted = jax.random.randint(jax.random.fold_in(rng, 1), (couples,), 0, 1 << 20) % (room + 1)
    lengths = lengths.at[1:1 + 2 * couples:2].set(donor - shifted).at[2:2 + 2 * couples:2].set(taker + shifted)
    return lengths[jax.random.permutation(jax.random.fold_in(rng, 2), number_of)]


def bell_draw(key, extent, width, limit, split=(), held_as=jnp.bfloat16):
    drawn = jax.random.normal(key, extent, jnp.float32) * width
    if len(split) > 0:
        drawn = levels(key, extent, split, -0.22, 0.18) * drawn
    return jnp.clip(drawn, min=-limit, max=limit).astype(held_as)


def heavy_noise(own_key, shape, scale, bound, shards, heavy, kind=jnp.bfloat16):
    drawn = scale * jax.random.normal(own_key, shape, jnp.float32)
    if shards:
        drawn = drawn * levels(own_key, shape, shards, -0.22, 0.18)
    return jnp.clip(spiked(drawn, jax.random.fold_in(own_key, 3), *heavy), -bound, bound).astype(kind)


def setup_inputs(seed: int = 0) -> dict:
    key_list = jax.random.split(jax.random.key(seed), 14)
    return {
        "tokens": heavy_noise(key_list[0], (SEQS, LEN, D), 1.0, 6.0, ((0, 16),), (0, 2, 16, 2.0)),
        "segment_ids": jax.vmap(lambda own: jnp.searchsorted(jnp.cumsum(uneven(own, 6, LEN, LEN // 4, 0)), jnp.arange(LEN), side="right"))(jax.random.split(key_list[1], SEQS)).reshape((SEQS, LEN)).astype(jnp.int32),
        "w_qkv": bell_draw(key_list[2], (D, 3, D), D ** -0.5, 0.21875, ((2, 2),)),
        "qv_bias": bell_draw(key_list[3], (2, D), 0.5, 3.0, ((1, 2),)),
        "w_out": bell_draw(key_list[4], (D, D), (D // 8) ** -0.5, 0.625, ((1, 2),)),
        "out_bias": bell_draw(key_list[5], (D,), 0.3, 2.0),
        "w_in": bell_draw(key_list[6], (D, FF), D ** -0.5, 0.21875, ((1, 2),)),
        "hidden_bias": bell_draw(key_list[7], (FF,), 0.5, 3.0, ((0, 2),)),
        "w_down": bell_draw(key_list[8], (D, FF), (FF // 2) ** -0.5, 0.15625, ((1, 2),)),
        "mlp_bias": bell_draw(key_list[9], (D,), 0.3, 2.0),
        "ln_gain": jnp.clip(1.0 + 0.1 * jax.random.normal(key_list[10], (2, D), jnp.float32), 0.5, 1.5).astype(jnp.bfloat16),
        "ln_bias": bell_draw(key_list[11], (2, D), 0.3, 2.0),
        "cotangent": heavy_noise(key_list[12], (SEQS, LEN, D), 1.0, 6.0, ((0, 16),), (0, 2, 16, 2.0)),
    }


norm_eps = 1e-06
masked_score = -1000000000.0

@jax.custom_vjp
def low(v):
    return lax.optimization_barrier(v.astype(jnp.bfloat16)).astype(jnp.float32)

@jax.custom_vjp
def low_back(v):
    return v

def low_keep(v):
    return (low(v), None)

def low_pass(kept, grad):
    return (grad,)

def back_keep(v):
    return (v, None)

def back_low(kept, grad):
    return (low(grad),)
low.defvjp(low_keep, low_pass)
low_back.defvjp(back_keep, back_low)

def layer_norm(values, gain, shift):
    center = values - lax.optimization_barrier(jnp.mean(values, axis=-1, keepdims=True))
    spread = lax.optimization_barrier(jnp.mean(center * center, axis=-1, keepdims=True))
    return center * lax.rsqrt(spread + norm_eps) * gain + shift

def forward_group(params, inputs, segments):
    w_qkv, qv_bias, w_out, out_bias, w_in, hidden_bias, w_down, mlp_bias, ln_gain, ln_bias = params
    highest = lax.Precision.HIGHEST
    group = inputs.shape[0]
    normed = low(layer_norm(inputs, ln_gain[0], ln_bias[0]))
    mixed = jnp.einsum('gld,dce->glce', normed, w_qkv, precision=highest)
    query = low_back(low(mixed[:, :, 0] + qv_bias[0])).reshape(group, LEN, HEADS, HEAD_DIM)
    keys = low_back(low(mixed[:, :, 1])).reshape(group, LEN, HEADS, HEAD_DIM)
    values = low_back(low(mixed[:, :, 2] + qv_bias[1])).reshape(group, LEN, HEADS, HEAD_DIM)
    scores = low_back(jnp.einsum('gqhe,gkhe->ghqk', query, keys, precision=highest) * HEAD_DIM ** (-0.5))
    allowed = segments[:, None, :, None] == segments[:, None, None, :]
    scores = jnp.where(allowed, scores, masked_score)
    top_score = lax.optimization_barrier(jnp.max(scores, axis=-1, keepdims=True))
    expo = jnp.exp(scores - top_score)
    weights = low(expo / lax.optimization_barrier(jnp.sum(expo, axis=-1, keepdims=True)))
    heads = jnp.einsum('ghqk,gkhe->gqhe', weights, values, precision=highest)
    heads = low_back(low(heads.reshape(group, LEN, N_TENSOR, D // N_TENSOR)))
    partials = jnp.einsum('glte,dte->tgld', heads, w_out.reshape(D, N_TENSOR, D // N_TENSOR), precision=highest)
    attended = low_back(lax.optimization_barrier(jnp.sum(low(partials), axis=0))) + out_bias
    resid = inputs + attended
    normed_two = low(layer_norm(resid, ln_gain[1], ln_bias[1]))
    hidden_pre = low_back(jnp.einsum('gld,df->glf', normed_two, w_in, precision=highest) + hidden_bias)
    active = low(jax.nn.gelu(hidden_pre, approximate=False))
    active = active.reshape(group, LEN, N_TENSOR, FF // N_TENSOR)
    partials_two = jnp.einsum('glte,dte->tgld', active, w_down.reshape(D, N_TENSOR, FF // N_TENSOR), precision=highest)
    mlp_result = low_back(lax.optimization_barrier(jnp.sum(low(partials_two), axis=0))) + mlp_bias
    return resid + mlp_result

def reference(tokens, segment_ids, w_qkv, qv_bias, w_out, out_bias, w_in, hidden_bias, w_down, mlp_bias, ln_gain, ln_bias, cotangent):
    grouped = math.gcd(SEQS, 16)
    steps_count = SEQS // grouped
    params = tuple((item.astype(jnp.float32) for item in (w_qkv, qv_bias, w_out, out_bias, w_in, hidden_bias, w_down, mlp_bias, ln_gain, ln_bias)))
    inputs = tokens.astype(jnp.float32)
    segments = segment_ids.reshape(steps_count, grouped, LEN)
    checked = jax.checkpoint(forward_group)

    def forward(weights, values):
        pieces = values.reshape(steps_count, grouped, LEN, D)
        outputs = lax.map(lambda pair: checked(weights, pair[0], pair[1]), (pieces, segments))
        return outputs.reshape(SEQS, LEN, D)
    result, pullback = jax.vjp(forward, params, inputs)
    grad_params, grad_inputs = pullback(cotangent.astype(jnp.float32))
    return (result.astype(jnp.bfloat16), grad_inputs.astype(jnp.bfloat16), grad_params[0], grad_params[1], grad_params[2], grad_params[3], grad_params[4], grad_params[5], grad_params[6], grad_params[7], grad_params[8], grad_params[9])
```

```python
import functools

import jax
import jax.numpy as jnp
from jax import lax
from jax.experimental import pallas as pl
from jax.experimental.pallas import tpu as pltpu
from jax.sharding import PartitionSpec as P

MESH = pl.DeviceIdType.MESH
BF = jnp.bfloat16
F32 = jnp.float32
HEAD = 64
NORM_EPS = 1e-06
MASKED = -1000000000.0
BITS = 4
WAYS = 2**BITS
CHUNK = 64
TILE = 384

NN = ((1,), (0,))
NT = ((1,), (1,))
TN = ((0,), (0,))


def dot(a, b, dims):
    return lax.dot_general(a, b, (dims, ((), ())), preferred_element_type=F32)


def loop(count, step):
    def run(i, carry):
        step(i)
        return carry

    lax.fori_loop(0, count, run, 0)


def cols(i, width):
    return pl.ds(pl.multiple_of(i * width, width), width)


def rows(i, height):
    return pl.ds(pl.multiple_of(i * height, height), height)


def kernel(
    stride,
    tok_h,
    seg_ref,
    wqkv_h,
    wout_h,
    win_h,
    wdn_h,
    vin,
    dy_h,
    block_h,
    gtok_h,
    gqkv_ref,
    gout_ref,
    gin_ref,
    gdn_ref,
    vout,
    tok,
    dy,
    wq,
    wo,
    win,
    wdn,
    a_buf,
    xh1,
    r1,
    qkv,
    p_buf,
    o_buf,
    h_buf,
    xh2,
    r2,
    c_buf,
    g_buf,
    du_buf,
    dc_snd,
    dc_rcv,
    mlp_snd,
    mlp_rcv,
    da_snd,
    da_rcv,
    do_buf,
    dhb,
    dp_buf,
    out_buf,
    l_t,
    grads,
    r0_buf,
    r1_buf,
    r2_buf,
    r3_buf,
    vacc,
    vrcv,
    in_sem,
    wo_send,
    wo_recv,
    x_send,
    x_recv,
    g_send,
    g_recv,
    v_send,
    v_recv,
    out_sem,
):
    d = lax.axis_index("dp")
    t = lax.axis_index("tensor")
    group = d // stride
    bit = [lax.rem(group // (2**b), 2) for b in range(BITS)]
    mate = [d + (1 - 2 * bit[b]) * (2**b) * stride for b in range(BITS)]
    seqs, length, width = 2, 256, tok.shape[-1]
    half = wo.shape[1] // 2
    pairs = wo.shape[2] // (2 * HEAD)
    hidden = win.shape[1]
    scale = HEAD ** (-0.5)

    loads = []

    def load(src, dst):
        copy = pltpu.make_async_copy(src, dst, in_sem.at[len(loads)])
        copy.start()
        loads.append(copy)
        return copy

    tok_load = load(tok_h, tok)
    wq_loads = [
        load(
            wqkv_h.at[kind, :, p * 128 : (p + 1) * 128],
            wq.at[:, p * 384 + kind * 128 : p * 384 + (kind + 1) * 128],
        )
        for p in range(pairs)
        for kind in range(3)
    ]
    wo_load = load(wout_h, wo.at[t])
    win_load = load(win_h, win)
    wdn_load = load(wdn_h, wdn)
    dy_load = load(dy_h, dy)

    barrier = pltpu.get_barrier_semaphore()
    pl.semaphore_signal(barrier, inc=1, device_id=(d, 1 - t), device_id_type=MESH)
    for b in range(BITS):
        pl.semaphore_signal(barrier, inc=1, device_id=(mate[b], t), device_id_type=MESH)
    pl.semaphore_wait(barrier, BITS + 1)

    def across(src, dst, send, recv):
        return pltpu.make_async_remote_copy(
            src_ref=src,
            dst_ref=dst,
            send_sem=send,
            recv_sem=recv,
            device_id=(d, 1 - t),
            device_id_type=MESH,
        )

    def toward(b, src, dst, send, recv):
        return pltpu.make_async_remote_copy(
            src_ref=src,
            dst_ref=dst,
            send_sem=send,
            recv_sem=recv,
            device_id=(mate[b], t),
            device_id_type=MESH,
        )

    part = pl.ds(pl.multiple_of(bit[0] * half, half), half)
    wo_first = across(wout_h.at[part], wo.at[t, part], wo_send.at[0], wo_recv.at[0])
    wo_second = toward(
        0, wo.at[1 - t, part], wo.at[1 - t, part], wo_send.at[1], wo_recv.at[1]
    )
    wo_first.start()

    def o_copy(s):
        return across(
            o_buf.at[t, rows(s, length)],
            o_buf.at[t, rows(s, length)],
            x_send.at[0, s],
            x_recv.at[0, s],
        )

    def x_copy(kind, snd, rcv, s):
        here = rows(s, length)
        return across(snd.at[here], rcv.at[here], x_send.at[kind, s], x_recv.at[kind, s])

    def dc_copy(s):
        return x_copy(1, dc_snd, dc_rcv, s)

    def mlp_copy(s):
        return x_copy(2, mlp_snd, mlp_rcv, s)

    def da_copy(s):
        return x_copy(3, da_snd, da_rcv, s)

    vacc[...] = jnp.zeros_like(vacc)

    lane = lax.broadcasted_iota(jnp.int32, (1, 128), 1)
    low_half = lane < HEAD

    def stacked(value):
        zero = jnp.zeros_like(value)
        return jnp.concatenate(
            [jnp.where(low_half, value, zero), jnp.where(low_half, zero, value)], axis=0
        )

    def normalize(value):
        mean = jnp.sum(value, axis=-1, keepdims=True) * (1.0 / width)
        center = value - mean
        spread = jnp.sum(center * center, axis=-1, keepdims=True) * (1.0 / width)
        scale_back = lax.rsqrt(spread + NORM_EPS)
        return center * scale_back, scale_back

    def norm_back(grad, normed, scale_back, gain):
        inner = grad * gain
        mean_one = jnp.sum(inner, axis=-1, keepdims=True) * (1.0 / width)
        mean_two = jnp.sum(inner * normed, axis=-1, keepdims=True) * (1.0 / width)
        return scale_back * (inner - mean_one - normed * mean_two)

    def same_image(s):
        ids = jnp.where(s == 0, seg_ref[0:1], seg_ref[1:2]).astype(F32)
        down = jnp.broadcast_to(ids, (128, length)).T
        return jnp.concatenate(
            [down == ids[:, i * 128 : (i + 1) * 128] for i in range(length // 128)], axis=1
        )

    tok_load.wait()
    for copy in wq_loads:
        copy.wait()

    def forward_one(s):
        def norm_step(i):
            here = rows(s * (length // CHUNK) + i, CHUNK)
            normed, scale_back = normalize(tok[here].astype(F32))
            xh1[here] = normed
            r1[here] = scale_back
            a_buf[here] = (normed * vin[0:1] + vin[2:3]).astype(BF)

        loop(length // CHUNK, norm_step)
        seq = rows(s, length)
        allowed = same_image(s)

        def pair_step(p):
            bias = jnp.concatenate(
                [
                    vin[8:9, cols(p, 128)],
                    jnp.zeros((1, 128), F32),
                    vin[8:9, pl.ds(pl.multiple_of(pairs * 128 + p * 128, 128), 128)],
                ],
                axis=1,
            )
            mixed = (dot(a_buf[seq], wq[:, cols(p, 384)], NN) + bias).astype(BF)
            qkv[seq, cols(p, 384)] = mixed
            scores = dot(mixed[:, :128], stacked(mixed[:, 128:256]), NT) * scale
            soft = []
            for e in range(2):
                one = jnp.where(allowed, scores[:, e * length : (e + 1) * length], MASKED)
                expo = jnp.exp(one - jnp.max(one, axis=-1, keepdims=True))
                soft.append(expo * (1.0 / jnp.sum(expo, axis=-1, keepdims=True)))
            both = jnp.concatenate(soft, axis=1)
            p_buf[s * pairs + p] = both
            o_buf[t, seq, cols(p, 128)] = dot(
                both.astype(BF), stacked(mixed[:, 256:]), NN
            ).astype(BF)

        loop(pairs, pair_step)
        o_copy(s).start()

    loop(seqs, forward_one)

    wo_first.wait_recv()
    wo_second.start()
    wo_load.wait()
    win_load.wait()
    wdn_load.wait()
    dy_load.wait()
    wo_second.wait_recv()

    def middle_one(s):
        seq = rows(s, length)
        o_copy(s).wait_recv()
        h_buf[seq] = dot(o_buf[0, seq], wo[0], NT) + dot(o_buf[1, seq], wo[1], NT)

        def norm_step(i):
            here = rows(s * (length // CHUNK) + i, CHUNK)
            resid = h_buf[here] + vin[4:5] + tok[here].astype(F32)
            h_buf[here] = resid
            normed, scale_back = normalize(resid)
            xh2[here] = normed
            r2[here] = scale_back
            c_buf[here] = (normed * vin[1:2] + vin[3:4]).astype(BF)

        loop(length // CHUNK, norm_step)

        for n in range(2):
            size = hidden // 2

            def hidden_step(i, n=n, size=size):
                here = pl.ds(pl.multiple_of(n * size + i * 256, 256), 256)
                there = cols(i, 256)
                pre = dot(c_buf[seq], win[:, here], NN) + vin[6 + n : 7 + n, there]
                back = dot(dy[seq], wdn[:, here], NN)
                phi = 0.5 + 0.5 * lax.erf(pre * 0.7071067811865476)
                g_buf[seq, here] = (pre * phi).astype(BF)
                slope = phi + pre * (jnp.exp(-0.5 * pre * pre) * 0.3989422804014327)
                low = (back * slope).astype(BF)
                du_buf[seq, here] = low
                vacc[1 + n : 2 + n, there] += jnp.sum(low.astype(F32), axis=0, keepdims=True)

            loop(size // 256, hidden_step)

        def back_step(i):
            here = cols(i, 256)
            grad = dot(du_buf[seq], win[rows(i, 256)], NT)
            dc_snd[seq, here] = grad.astype(BF)
            vacc[6:7, here] += jnp.sum(grad * xh2[seq, here], axis=0, keepdims=True)
            vacc[8:9, here] += jnp.sum(grad, axis=0, keepdims=True)

        loop(width // 256, back_step)
        dc_copy(s).start()

    loop(seqs, middle_one)

    def turn(src):
        for s in range(seqs):
            l_t[:, s * length : (s + 1) * length] = src[s * length : (s + 1) * length].T

    strip = width // WAYS

    def product(piece, right):
        full = dot(l_t[...], right, NN)
        for k in range(WAYS):
            b = [(k >> i) & 1 for i in range(BITS)]
            grads[piece, b[0], b[1], b[2], b[3]] = full[k * strip : (k + 1) * strip].astype(BF)

    received = [r0_buf, r1_buf, r2_buf, r3_buf]

    def own(piece, depth):
        return (piece,) + tuple(bit[:depth])

    def g_copy(piece, k):
        return toward(
            k,
            grads.at[own(piece, k) + (1 - bit[k],)],
            received[k].at[piece],
            g_send.at[piece, k],
            g_recv.at[piece, k],
        )

    def pass_on(piece, k):
        g_copy(piece, k).wait_recv()
        here = own(piece, k + 1)
        grads[here] = (grads[here].astype(F32) + received[k][piece].astype(F32)).astype(BF)
        g_copy(piece, k + 1).start()

    def finish(piece):
        g_copy(piece, 3).wait_recv()
        return grads[own(piece, 4)].astype(F32) + received[3][piece].astype(F32)

    hidden_pieces = hidden // TILE
    down, into, outs, mixes = 0, hidden_pieces, 2 * hidden_pieces, 2 * hidden_pieces + 1
    total = mixes + pairs

    turn(dy)

    def down_step(i):
        product(down + i, g_buf[:, cols(i, TILE)])
        g_copy(down + i, 0).start()

    loop(hidden_pieces, down_step)
    vacc[4:5] += jnp.sum(dy[...].astype(F32), axis=0, keepdims=True)

    def mlp_out(s):
        seq = rows(s, length)

        def step(i):
            mlp_snd[seq, cols(i, 256)] = dot(g_buf[seq], wdn[rows(i, 256)], NT).astype(BF)

        loop(width // 256, step)
        mlp_copy(s).start()

    def resid_back(s):
        seq = rows(s, length)
        dc_copy(s).wait_recv()

        def step(i):
            here = rows(s * (length // CHUNK) + i, CHUNK)
            grad = dc_snd[here].astype(F32) + dc_rcv[here].astype(F32)
            full = dy[here].astype(F32) + norm_back(grad, xh2[here], r2[here], vin[1:2])
            xh2[here] = full
            dhb[here] = full.astype(BF)
            vacc[3:4] += jnp.sum(full, axis=0, keepdims=True)

        loop(length // CHUNK, step)
        do_buf[seq] = dot(dhb[seq], wo[t], NN).astype(BF)

    def attention_back(s, p):
        seq = rows(s, length)
        mixed = qkv[seq, cols(p, 384)]
        query, keys = mixed[:, :128], stacked(mixed[:, 128:256])
        grad_o = do_buf[seq, cols(p, 128)]
        soft = p_buf[s * pairs + p]
        grad_soft = dot(grad_o, stacked(mixed[:, 256:]), NT)
        parts = []
        for e in range(2):
            one, two = (v[:, e * length : (e + 1) * length] for v in (soft, grad_soft))
            delta = jnp.sum(one * two, axis=-1, keepdims=True)
            parts.append((one * (two - delta)).astype(BF))
        grad_scores = jnp.concatenate(parts, axis=1)
        grad_query = dot(grad_scores, keys, NN) * scale
        grad_keys = dot(grad_scores, query, TN) * scale
        grad_keys = jnp.where(low_half, grad_keys[:length], grad_keys[length:])
        grad_values = dot(soft.astype(BF), grad_o, TN)
        grad_values = jnp.where(low_half, grad_values[:length], grad_values[length:])
        low = [v.astype(BF) for v in (grad_query, grad_keys, grad_values)]
        dp_buf[seq, cols(p, 384)] = jnp.concatenate(low, axis=1)
        vacc[0:1, cols(p, 128)] += jnp.sum(low[0].astype(F32), axis=0, keepdims=True)
        vacc[0:1, pl.ds(pl.multiple_of(pairs * 128 + p * 128, 128), 128)] += jnp.sum(
            low[2].astype(F32), axis=0, keepdims=True
        )

    def mixed_back(s):
        seq = rows(s, length)

        def step(i):
            here = cols(i, 256)
            grad = dot(dp_buf[seq], wq[rows(i, 256)], NT)
            da_snd[seq, here] = grad.astype(BF)
            vacc[5:6, here] += jnp.sum(grad * xh1[seq, here], axis=0, keepdims=True)
            vacc[7:8, here] += jnp.sum(grad, axis=0, keepdims=True)

        loop(width // 256, step)
        da_copy(s).start()

    resid_back(0)
    loop(hidden_pieces, lambda i: pass_on(down + i, 0))
    mlp_out(0)
    loop(pairs, lambda p: attention_back(0, p))
    mixed_back(0)

    turn(c_buf)

    def into_step(i):
        product(into + i, du_buf[:, cols(i, TILE)])
        g_copy(into + i, 0).start()

    loop(hidden_pieces, into_step)
    loop(hidden_pieces, lambda i: pass_on(down + i, 1))

    resid_back(1)
    loop(hidden_pieces, lambda i: pass_on(into + i, 0))
    turn(dhb)
    product(outs, o_buf[t])
    g_copy(outs, 0).start()
    loop(hidden_pieces, lambda i: pass_on(down + i, 2))

    turn(a_buf)

    def last_step(p):
        attention_back(1, p)
        product(mixes + p, dp_buf[:, cols(p, 384)])
        g_copy(mixes + p, 0).start()

    loop(pairs, last_step)
    mixed_back(1)
    pass_on(outs, 0)
    loop(pairs, lambda p: pass_on(mixes + p, 0))
    mlp_out(1)

    def v_copy(k):
        if k == BITS:
            return across(vacc_at(k), vrcv.at[k], v_send.at[k], v_recv.at[k])
        return toward(k, vacc_at(k), vrcv.at[k], v_send.at[k], v_recv.at[k])

    def vacc_at(k):
        return vsum.at[k]

    vsum = vout.at[1:]
    vsum[0] = vacc[...]
    v_copy(0).start()

    def v_next(k):
        v_copy(k).wait_recv()
        vsum[k + 1] = vsum[k] + vrcv[k]
        v_copy(k + 1).start()

    loop(hidden_pieces, lambda i: pass_on(into + i, 1))
    v_next(0)
    loop(hidden_pieces, lambda i: pass_on(into + i, 2))

    def down_out(i):
        gdn_ref[:, cols(i, TILE)] = finish(down + i)

    def into_out(i):
        gin_ref[:, cols(i, TILE)] = finish(into + i)

    loop(hidden_pieces, down_out)
    pass_on(outs, 1)
    v_next(1)

    def finish_block(s):
        mlp_copy(s).wait_recv()

        def step(i):
            here = rows(s * (length // CHUNK) + i, CHUNK)
            added = mlp_snd[here].astype(F32) + mlp_rcv[here].astype(F32)
            out_buf[0, here] = (h_buf[here] + (added + vin[5:6])).astype(BF)

        loop(length // CHUNK, step)
        out_copy(0, block_h, s).start()

    def out_copy(n, dst, s):
        here = rows(s, length)
        return pltpu.make_async_copy(out_buf.at[n, here], dst.at[here], out_sem.at[n, s])

    def finish_tokens(s):
        da_copy(s).wait_recv()

        def step(i):
            here = rows(s * (length // CHUNK) + i, CHUNK)
            grad = da_snd[here].astype(F32) + da_rcv[here].astype(F32)
            full = xh2[here] + norm_back(grad, xh1[here], r1[here], vin[0:1])
            out_buf[1, here] = full.astype(BF)

        loop(length // CHUNK, step)
        out_copy(1, gtok_h, s).start()

    finish_block(0)
    finish_tokens(0)
    loop(pairs, lambda p: pass_on(mixes + p, 1))
    v_next(2)
    pass_on(outs, 2)
    loop(hidden_pieces, into_out)
    loop(pairs, lambda p: pass_on(mixes + p, 2))
    v_next(3)
    gout_ref[...] = finish(outs)
    finish_tokens(1)
    finish_block(1)

    def mix_out(p):
        value = finish(mixes + p)
        for kind in range(3):
            gqkv_ref[kind, :, cols(p, 128)] = value[:, kind * 128 : (kind + 1) * 128]

    loop(pairs, mix_out)

    v_copy(BITS).wait_recv()
    line = lax.broadcasted_iota(jnp.int32, vacc.shape, 0)
    norms = (line >= 5) & (line < 9)
    final = vsum[BITS]
    vout[0] = jnp.where(norms, final + vrcv[BITS], final)

    wo_first.wait_send()
    wo_second.wait_send()
    for s in range(seqs):
        o_copy(s).wait_send()
        dc_copy(s).wait_send()
        mlp_copy(s).wait_send()
        da_copy(s).wait_send()
        out_copy(0, block_h, s).wait()
        out_copy(1, gtok_h, s).wait()

    def sent(i):
        for k in range(BITS):
            g_copy(i, k).wait_send()

    loop(total, sent)
    for k in range(BITS + 1):
        v_copy(k).wait_send()


def body(
    tokens,
    segment_ids,
    w_qkv,
    qv_bias,
    w_out,
    out_bias,
    w_in,
    hidden_bias,
    w_down,
    mlp_bias,
    ln_gain,
    ln_bias,
    cotangent,
    *,
    dp,
):
    seqs, length, width = tokens.shape
    count = seqs * length
    local = w_qkv.shape[2]
    hidden = w_in.shape[1]
    pairs = local // (2 * HEAD)
    stride = dp // WAYS
    strip = width // WAYS
    pieces = 2 * (hidden // TILE) + 1 + pairs
    lines = jnp.concatenate(
        [
            ln_gain.astype(F32),
            ln_bias.astype(F32),
            out_bias.astype(F32)[None],
            mlp_bias.astype(F32)[None],
            hidden_bias.astype(F32).reshape(2, width),
            qv_bias.astype(F32).reshape(1, width),
            jnp.zeros((7, width), F32),
        ],
        axis=0,
    )
    hbm = pl.BlockSpec(memory_space=pl.ANY)
    vmem = pl.BlockSpec(memory_space=pltpu.VMEM)
    dma = pltpu.SemaphoreType.DMA
    wide = (count, width)
    outs = pl.pallas_call(
        functools.partial(kernel, stride),
        out_shape=(
            jax.ShapeDtypeStruct(wide, BF),
            jax.ShapeDtypeStruct(wide, BF),
            jax.ShapeDtypeStruct((3, strip, local), F32),
            jax.ShapeDtypeStruct((strip, local), F32),
            jax.ShapeDtypeStruct((strip, hidden), F32),
            jax.ShapeDtypeStruct((strip, hidden), F32),
            jax.ShapeDtypeStruct((BITS + 2, 16, width), F32),
        ),
        in_specs=[hbm, vmem, hbm, hbm, hbm, hbm, vmem, hbm],
        out_specs=(hbm, hbm, vmem, vmem, vmem, vmem, vmem),
        scratch_shapes=[
            pltpu.VMEM(wide, BF),
            pltpu.VMEM(wide, BF),
            pltpu.VMEM((width, 3 * local), BF),
            pltpu.VMEM((2, width, local), BF),
            pltpu.VMEM((width, hidden), BF),
            pltpu.VMEM((width, hidden), BF),
            pltpu.VMEM(wide, BF),
            pltpu.VMEM(wide, F32),
            pltpu.VMEM((count, 1), F32),
            pltpu.VMEM((count, 3 * local), BF),
            pltpu.VMEM((seqs * pairs, length, 2 * length), F32),
            pltpu.VMEM((2, count, local), BF),
            pltpu.VMEM(wide, F32),
            pltpu.VMEM(wide, F32),
            pltpu.VMEM((count, 1), F32),
            pltpu.VMEM(wide, BF),
            pltpu.VMEM((count, hidden), BF),
            pltpu.VMEM((count, hidden), BF),
            pltpu.VMEM(wide, BF),
            pltpu.VMEM(wide, BF),
            pltpu.VMEM(wide, BF),
            pltpu.VMEM(wide, BF),
            pltpu.VMEM(wide, BF),
            pltpu.VMEM(wide, BF),
            pltpu.VMEM((count, local), BF),
            pltpu.VMEM(wide, BF),
            pltpu.VMEM((count, 3 * local), BF),
            pltpu.VMEM((2, count, width), BF),
            pltpu.VMEM((width, count), BF),
            pltpu.VMEM((pieces, 2, 2, 2, 2, strip, TILE), BF),
            pltpu.VMEM((pieces, 2, 2, 2, strip, TILE), BF),
            pltpu.VMEM((pieces, 2, 2, strip, TILE), BF),
            pltpu.VMEM((pieces, 2, strip, TILE), BF),
            pltpu.VMEM((pieces, strip, TILE), BF),
            pltpu.VMEM((16, width), F32),
            pltpu.VMEM((BITS + 1, 16, width), F32),
            dma((5 + 3 * pairs,)),
            dma((2,)),
            dma((2,)),
            dma((4, seqs)),
            dma((4, seqs)),
            dma((pieces, BITS)),
            dma((pieces, BITS)),
            dma((BITS + 1,)),
            dma((BITS + 1,)),
            dma((2, seqs)),
        ],
        compiler_params=pltpu.CompilerParams(
            collective_id=0, has_side_effects=True, vmem_limit_bytes=60 * 2**20
        ),
        cost_estimate=pl.CostEstimate(
            flops=12 * 10**9, bytes_accessed=12 * 10**6, transcendentals=4 * 10**6
        ),
    )(
        tokens.reshape(wide),
        segment_ids,
        w_qkv.transpose(1, 0, 2),
        w_out,
        w_in,
        w_down,
        lines,
        cotangent.reshape(wide),
    )
    block, grad_tokens, gqkv, gout, gin, gdn, small = outs
    small = small[0]
    gqkv = gqkv.transpose(1, 0, 2)
    if stride > 1:
        groups = [[g * stride + i for i in range(stride)] for g in range(WAYS)]
        gqkv, gout, gin, gdn = (
            lax.psum_scatter(v, "dp", scatter_dimension=0, axis_index_groups=groups, tiled=True)
            for v in (gqkv, gout, gin, gdn)
        )
        small = lax.psum(small, "dp", axis_index_groups=groups)
    return (
        block.reshape(tokens.shape),
        grad_tokens.reshape(tokens.shape),
        gqkv,
        small[0].reshape(2, local),
        gout,
        small[3],
        gin,
        small[1:3].reshape(hidden),
        gdn,
        small[4],
        small[5:7],
        small[7:9],
    )


def solution(mesh):
    return jax.shard_map(
        functools.partial(body, dp=mesh.shape["dp"]),
        mesh=mesh,
        in_specs=(
            P("dp", None, None),
            P("dp", None),
            P(None, None, "tensor"),
            P(None, "tensor"),
            P(None, "tensor"),
            P(),
            P(None, "tensor"),
            P("tensor"),
            P(None, "tensor"),
            P(),
            P(),
            P(),
            P("dp", None, None),
        ),
        out_specs=(
            P("dp", None, None),
            P("dp", None, None),
            P("dp", None, "tensor"),
            P(None, "tensor"),
            P("dp", "tensor"),
            P(),
            P("dp", "tensor"),
            P("tensor"),
            P("dp", "tensor"),
            P(),
            P(),
            P(),
        ),
        check_vma=False,
    )
```

```python
import functools

import jax
import jax.numpy as jnp
from jax import lax
from jax.experimental import pallas as pl
from jax.experimental.pallas import tpu as pltpu
from jax.sharding import PartitionSpec as P

MESH = pl.DeviceIdType.MESH
BF = jnp.bfloat16
F32 = jnp.float32
HEAD = 64
NORM_EPS = 1e-06
MASKED = -1000000000.0
BITS = 4
WAYS = 2**BITS
BLOCK = 256
CHUNK = 64
TILE = 384

NN = ((1,), (0,))
NT = ((1,), (1,))
TN = ((0,), (0,))


def dot(a, b, dims):
    return lax.dot_general(a, b, (dims, ((), ())), preferred_element_type=F32)


def loop(count, step):
    def run(i, carry):
        step(i)
        return carry

    lax.fori_loop(0, count, run, 0)


def cols(i, width):
    return pl.ds(pl.multiple_of(i * width, width), width)


def rows(i, height):
    return pl.ds(pl.multiple_of(i * height, height), height)


def kernel(
    stride,
    tok_h,
    seg_ref,
    wqkv_h,
    qvb_ref,
    wout_h,
    ob_ref,
    win_h,
    hb_ref,
    wdn_h,
    mb_ref,
    gain_ref,
    shift_ref,
    dy_h,
    block_h,
    gtok_h,
    gqkv_ref,
    gout_ref,
    gin_ref,
    gdn_ref,
    vout,
    tok,
    dy,
    wq,
    wo,
    win,
    wdn,
    vin,
    a_buf,
    xh1,
    r1,
    qkv,
    p_buf,
    o_buf,
    h_buf,
    xh2,
    r2,
    c_buf,
    g_buf,
    du_buf,
    dc_snd,
    dc_rcv,
    mlp_snd,
    mlp_rcv,
    da_snd,
    da_rcv,
    do_buf,
    dhb,
    dp_buf,
    out_buf,
    l_t,
    grads,
    r0_buf,
    r1_buf,
    r2_buf,
    r3_buf,
    vsum,
    vrcv,
    in_sem,
    wo_send,
    wo_recv,
    o_send,
    o_recv,
    x_send,
    x_recv,
    g_send,
    g_recv,
    v_send,
    v_recv,
    out_sem,
):
    d = lax.axis_index("dp")
    t = lax.axis_index("tensor")
    group = d // stride
    bit = [lax.rem(group // (2**b), 2) for b in range(BITS)]
    mate = [d + (1 - 2 * bit[b]) * (2**b) * stride for b in range(BITS)]
    count, width = tok.shape
    seqs = seg_ref.shape[0]
    length = count // seqs
    local = wo.shape[2]
    pairs = local // (2 * HEAD)
    hidden = win.shape[1]
    scale = HEAD ** (-0.5)
    blocks = count // BLOCK
    vacc = vsum.at[0]

    barrier = pltpu.get_barrier_semaphore()
    pl.semaphore_signal(barrier, inc=1, device_id=(d, 1 - t), device_id_type=MESH)
    for b in range(BITS):
        pl.semaphore_signal(barrier, inc=1, device_id=(mate[b], t), device_id_type=MESH)

    loads = []

    def load(src, dst):
        copy = pltpu.make_async_copy(src, dst, in_sem.at[len(loads)])
        copy.start()
        loads.append(copy)
        return copy

    tok_load = load(tok_h, tok)
    wq_loads = [
        load(
            wqkv_h.at[kind, :, p * 128 : (p + 1) * 128],
            wq.at[:, p * 384 + kind * 128 : p * 384 + (kind + 1) * 128],
        )
        for p in range(pairs)
        for kind in range(3)
    ]
    dy_load = load(dy_h, dy)
    wo_load = load(wout_h, wo.at[t])
    win_load = load(win_h, win)
    wdn_load = load(wdn_h, wdn)

    def across(src, dst, send, recv):
        return pltpu.make_async_remote_copy(
            src_ref=src,
            dst_ref=dst,
            send_sem=send,
            recv_sem=recv,
            device_id=(d, 1 - t),
            device_id_type=MESH,
        )

    def toward(b, src, dst, send, recv):
        return pltpu.make_async_remote_copy(
            src_ref=src,
            dst_ref=dst,
            send_sem=send,
            recv_sem=recv,
            device_id=(mate[b], t),
            device_id_type=MESH,
        )

    slab = width // 8

    def wo_rows(turned, part):
        first = bit[0]
        second = 1 - bit[1] if turned else bit[1]
        return rows((2 * second + first) * 2 + part, slab)

    def wo_copy(step, part):
        sems = wo_send.at[step, part], wo_recv.at[step, part]
        if step == 0:
            here = wo_rows(False, part)
            return across(wout_h.at[here], wo.at[t, here], *sems)
        here = wo_rows(step == 3, part)
        return toward(1 if step == 2 else 0, wo.at[1 - t, here], wo.at[1 - t, here], *sems)

    def wo_share(part):
        wo_copy(0, part).wait_recv()
        wo_copy(2, part).start()
        wo_copy(1, part).start()

    def wo_forward(part):
        wo_copy(2, part).wait_recv()
        wo_copy(3, part).start()

    def o_copy(s, p):
        here = rows(s, length)
        place = o_buf.at[t, here, cols(p, 128)]
        return across(place, place, o_send.at[s, p], o_recv.at[s, p])

    def dc_copy(n, i):
        here = rows(n, BLOCK), cols(i, 256)
        return across(
            dc_snd.at[here], dc_rcv.at[here], x_send.at[0, n, i], x_recv.at[0, n, i]
        )

    def da_copy(s, i):
        here = rows(s, length), cols(i, 256)
        return across(
            da_snd.at[here], da_rcv.at[here], x_send.at[1, s, i], x_recv.at[1, s, i]
        )

    def mlp_copy(s, i):
        here = rows(s, length), cols(i, 256)
        return across(
            mlp_snd.at[here], mlp_rcv.at[here], x_send.at[2, s, i], x_recv.at[2, s, i]
        )

    wide = width // 256

    vacc[...] = jnp.zeros(vacc.shape, F32)
    vin[0:2] = gain_ref[...].astype(F32)
    vin[2:4] = shift_ref[...].astype(F32)
    vin[4:5] = ob_ref[...].astype(F32).reshape(1, width)
    vin[5:6] = mb_ref[...].astype(F32).reshape(1, width)
    line = hb_ref[...].astype(F32).reshape(1, hidden)
    vin[6:7] = line[:, :width]
    vin[7:8] = line[:, width:]
    vin[8:9, :local] = qvb_ref[0:1].astype(F32)
    vin[8:9, local:] = qvb_ref[1:2].astype(F32)

    lane = lax.broadcasted_iota(jnp.int32, (1, 128), 1)
    low_half = lane < HEAD

    def stacked(value):
        zero = jnp.zeros_like(value)
        return jnp.concatenate(
            [jnp.where(low_half, value, zero), jnp.where(low_half, zero, value)], axis=0
        )

    def normalize(value):
        mean = jnp.sum(value, axis=-1, keepdims=True) * (1.0 / width)
        center = value - mean
        spread = jnp.sum(center * center, axis=-1, keepdims=True) * (1.0 / width)
        scale_back = lax.rsqrt(spread + NORM_EPS)
        return center * scale_back, scale_back

    def norm_back(grad, normed, scale_back, gain):
        inner = grad * gain
        mean_one = jnp.sum(inner, axis=-1, keepdims=True) * (1.0 / width)
        mean_two = jnp.sum(inner * normed, axis=-1, keepdims=True) * (1.0 / width)
        return scale_back * (inner - mean_one - normed * mean_two)

    def same_image(s):
        ids = seg_ref[s : s + 1].astype(F32)
        down = jnp.broadcast_to(ids, (128, length)).T
        return jnp.concatenate(
            [down == ids[:, i * 128 : (i + 1) * 128] for i in range(length // 128)], axis=1
        )

    def norm_one(s):
        def step(i):
            here = rows(s * (length // CHUNK) + i, CHUNK)
            normed, scale_back = normalize(tok[here].astype(F32))
            xh1[here] = normed
            r1[here] = scale_back
            a_buf[here] = (normed * vin[0:1] + vin[2:3]).astype(BF)

        loop(length // CHUNK, step)

    def attention(s):
        seq = rows(s, length)
        allowed = same_image(s)

        def pair_step(p):
            bias = jnp.concatenate(
                [
                    vin[8:9, cols(p, 128)],
                    jnp.zeros((1, 128), F32),
                    vin[8:9, cols(pairs + p, 128)],
                ],
                axis=1,
            )
            mixed = (dot(a_buf[seq], wq[:, cols(p, 384)], NN) + bias).astype(BF)
            qkv[seq, cols(p, 384)] = mixed
            scores = dot(mixed[:, :128], stacked(mixed[:, 128:256]), NT) * scale
            soft = []
            for e in range(2):
                one = jnp.where(allowed, scores[:, e * length : (e + 1) * length], MASKED)
                expo = jnp.exp(one - jnp.max(one, axis=-1, keepdims=True))
                soft.append(expo * (1.0 / jnp.sum(expo, axis=-1, keepdims=True)))
            both = jnp.concatenate(soft, axis=1)
            p_buf[s * pairs + p] = both
            o_buf[t, seq, cols(p, 128)] = dot(
                both.astype(BF), stacked(mixed[:, 256:]), NN
            ).astype(BF)
            o_copy(s, p).start()

        loop(pairs, pair_step)

    tok_load.wait()
    norm_one(0)
    pl.semaphore_wait(barrier, BITS + 1)
    wo_copy(0, 0).start()
    wo_copy(0, 1).start()
    for copy in wq_loads:
        copy.wait()
    attention(0)
    wo_share(0)
    norm_one(1)
    wo_share(1)
    attention(1)

    def turn(src):
        for s in range(seqs):
            l_t[:, s * length : (s + 1) * length] = src[s * length : (s + 1) * length].T

    strip = width // WAYS
    received = [r0_buf, r1_buf, r2_buf, r3_buf]

    def product(piece, right, order):
        full = dot(l_t[...], right, NN)
        for k in range(WAYS):
            b = [(k >> i) & 1 for i in order]
            grads[piece, b[0], b[1], b[2], b[3]] = full[k * strip : (k + 1) * strip].astype(BF)
        g_copy(piece, 0, order).start()

    def own(piece, depth, order):
        return (piece,) + tuple(bit[b] for b in order[:depth])

    def g_copy(piece, k, order):
        return toward(
            order[k],
            grads.at[own(piece, k, order) + (1 - bit[order[k]],)],
            received[k].at[piece],
            g_send.at[piece, k],
            g_recv.at[piece, k],
        )

    def pass_on(piece, k, order):
        g_copy(piece, k, order).wait_recv()
        here = own(piece, k + 1, order)
        grads[here] = (grads[here].astype(F32) + received[k][piece].astype(F32)).astype(BF)
        g_copy(piece, k + 1, order).start()

    def finish(piece, order):
        g_copy(piece, 3, order).wait_recv()
        return grads[own(piece, 4, order)].astype(F32) + received[3][piece].astype(F32)

    hidden_pieces = hidden // TILE
    down, into, outs, mixes = 0, hidden_pieces, 2 * hidden_pieces, 2 * hidden_pieces + 1
    total = mixes + pairs
    last = hidden_pieces - 1

    dy_load.wait()
    turn(dy)
    vacc[4:5] += jnp.sum(dy[...].astype(F32), axis=0, keepdims=True)
    wo_load.wait()
    win_load.wait()
    wdn_load.wait()
    for part in range(2):
        wo_forward(part)
    for part in range(2):
        wo_copy(1, part).wait_recv()
        wo_copy(3, part).wait_recv()

    per = length // BLOCK

    def middle(n):
        here = rows(n, BLOCK)

        @pl.when(lax.rem(n, per) == 0)
        def _():
            for p in range(pairs):
                o_copy(n // per, p).wait_recv()

        h_buf[here] = dot(o_buf[0, here], wo[0], NT) + dot(o_buf[1, here], wo[1], NT)

        def norm_step(i):
            few = rows(n * (BLOCK // CHUNK) + i, CHUNK)
            resid = h_buf[few] + vin[4:5] + tok[few].astype(F32)
            h_buf[few] = resid
            normed, scale_back = normalize(resid)
            xh2[few] = normed
            r2[few] = scale_back
            c_buf[few] = (normed * vin[1:2] + vin[3:4]).astype(BF)

        loop(BLOCK // CHUNK, norm_step)

        for m in range(hidden // width):

            def hidden_step(i, m=m):
                there = cols(i, 256)
                part = cols(m * wide + i, 256)
                pre = dot(c_buf[here], win[:, part], NN) + vin[6 + m : 7 + m, there]
                back = dot(dy[here], wdn[:, part], NN)
                phi = 0.5 + 0.5 * lax.erf(pre * 0.7071067811865476)
                g_buf[here, part] = (pre * phi).astype(BF)
                slope = phi + pre * (jnp.exp(-0.5 * pre * pre) * 0.3989422804014327)
                low = (back * slope).astype(BF)
                du_buf[here, part] = low
                vacc[1 + m : 2 + m, there] += jnp.sum(low.astype(F32), axis=0, keepdims=True)

            loop(wide, hidden_step)

        def back_step(i):
            there = cols(i, 256)
            grad = dot(du_buf[here], win[rows(i, 256)], NT)
            dc_snd[here, there] = grad.astype(BF)
            dc_copy(n, i).start()
            vacc[6:7, there] += jnp.sum(grad * xh2[here, there], axis=0, keepdims=True)
            vacc[8:9, there] += jnp.sum(grad, axis=0, keepdims=True)

        loop(wide, back_step)

    loop(blocks, middle)

    def mlp_out(s):
        seq = rows(s, length)

        def step(i):
            mlp_snd[seq, cols(i, 256)] = dot(g_buf[seq], wdn[rows(i, 256)], NT).astype(BF)
            mlp_copy(s, i).start()

        loop(wide, step)

    def resid_back(s):
        seq = rows(s, length)
        for n in range(s * per, (s + 1) * per):
            for i in range(wide):
                dc_copy(n, i).wait_recv()

        def step(i):
            here = rows(s * (length // CHUNK) + i, CHUNK)
            grad = dc_snd[here].astype(F32) + dc_rcv[here].astype(F32)
            full = dy[here].astype(F32) + norm_back(grad, xh2[here], r2[here], vin[1:2])
            xh2[here] = full
            dhb[here] = full.astype(BF)
            vacc[3:4] += jnp.sum(full, axis=0, keepdims=True)

        loop(length // CHUNK, step)
        do_buf[seq] = dot(dhb[seq], wo[t], NN).astype(BF)

    def attention_back(s, p):
        seq = rows(s, length)
        mixed = qkv[seq, cols(p, 384)]
        query, keys = mixed[:, :128], stacked(mixed[:, 128:256])
        grad_o = do_buf[seq, cols(p, 128)]
        soft = p_buf[s * pairs + p]
        grad_soft = dot(grad_o, stacked(mixed[:, 256:]), NT)
        parts = []
        for e in range(2):
            one, two = (v[:, e * length : (e + 1) * length] for v in (soft, grad_soft))
            delta = jnp.sum(one * two, axis=-1, keepdims=True)
            parts.append((one * (two - delta)).astype(BF))
        grad_scores = jnp.concatenate(parts, axis=1)
        grad_query = dot(grad_scores, keys, NN) * scale
        grad_keys = dot(grad_scores, query, TN) * scale
        grad_keys = jnp.where(low_half, grad_keys[:length], grad_keys[length:])
        grad_values = dot(soft.astype(BF), grad_o, TN)
        grad_values = jnp.where(low_half, grad_values[:length], grad_values[length:])
        low = [v.astype(BF) for v in (grad_query, grad_keys, grad_values)]
        dp_buf[seq, cols(p, 384)] = jnp.concatenate(low, axis=1)
        vacc[0:1, cols(p, 128)] += jnp.sum(low[0].astype(F32), axis=0, keepdims=True)
        vacc[0:1, cols(pairs + p, 128)] += jnp.sum(low[2].astype(F32), axis=0, keepdims=True)

    def mixed_back(s):
        seq = rows(s, length)

        def step(i):
            here = cols(i, 256)
            grad = dot(dp_buf[seq], wq[rows(i, 256)], NT)
            da_snd[seq, here] = grad.astype(BF)
            vacc[5:6, here] += jnp.sum(grad * xh1[seq, here], axis=0, keepdims=True)
            vacc[7:8, here] += jnp.sum(grad, axis=0, keepdims=True)

        loop(wide, step)

    def send_mixed(s):
        for i in range(wide):
            da_copy(s, i).start()

    def out_copy(n, dst, s):
        here = rows(s, length)
        return pltpu.make_async_copy(out_buf.at[n, here], dst.at[here], out_sem.at[n, s])

    def finish_block(s):
        seq = rows(s, length)

        def step(i):
            mlp_copy(s, i).wait_recv()
            here = seq, cols(i, 256)
            added = mlp_snd[here].astype(F32) + mlp_rcv[here].astype(F32)
            out_buf[0, seq, cols(i, 256)] = (h_buf[here] + (added + vin[5:6, cols(i, 256)])).astype(BF)

        loop(wide, step)
        out_copy(0, block_h, s).start()

    def finish_tokens(s):
        for i in range(wide):
            da_copy(s, i).wait_recv()

        def step(i):
            here = rows(s * (length // CHUNK) + i, CHUNK)
            grad = da_snd[here].astype(F32) + da_rcv[here].astype(F32)
            full = xh2[here] + norm_back(grad, xh1[here], r1[here], vin[0:1])
            out_buf[1, here] = full.astype(BF)

        loop(length // CHUNK, step)
        out_copy(1, gtok_h, s).start()

    def v_copy(k):
        sems = v_send.at[k], v_recv.at[k]
        if k == 0:
            return across(vsum.at[0], vrcv.at[0], *sems)
        return toward(k - 1, vsum.at[k], vrcv.at[k], *sems)

    def v_next(k):
        v_copy(k).wait_recv()
        if k == 0:
            line = lax.broadcasted_iota(jnp.int32, vacc.shape, 0)
            norms = (line >= 5) & (line < 9)
            vsum[1] = jnp.where(norms, vsum[0] + vrcv[0], vsum[0])
        else:
            vsum[k + 1] = vsum[k] + vrcv[k]
        if k < BITS:
            v_copy(k + 1).start()

    order_of = {}
    for piece in range(total):
        first_z = piece in (down + last, into + last, mixes + pairs - 1)
        order_of[piece] = (0, 2, 1, 3) if first_z else (0, 1, 2, 3)

    usual, turned = (0, 1, 2, 3), (0, 2, 1, 3)

    def passes(*what):
        for piece, k in what:
            pass_on(piece, k, order_of[piece])

    def wrap(p, size):
        return p[:, cols(size, TILE)]

    loop(last, lambda i: product(down + i, g_buf[:, cols(i, TILE)], usual))
    product(down + last, g_buf[:, last * TILE :], turned)
    turn(c_buf)

    def into_step(i):
        product(into + i, du_buf[:, cols(i, TILE)], usual)
        pass_on(down + i, 0, usual)

    loop(last, into_step)
    product(into + last, du_buf[:, last * TILE :], turned)
    pass_on(down + last, 0, turned)
    resid_back(0)
    loop(last, lambda i: pass_on(into + i, 0, usual))
    pass_on(into + last, 0, turned)
    loop(pairs, lambda p: attention_back(0, p))
    mixed_back(0)
    send_mixed(0)
    passes((down, 1), (down + 3, 1), (into + 3, 1))
    turn(a_buf)
    passes((down + 1, 1))
    resid_back(1)

    def last_step(p):
        attention_back(1, p)
        product(mixes + p, dp_buf[:, cols(p, 384)], usual)

    loop(pairs - 1, last_step)
    attention_back(1, pairs - 1)
    product(mixes + pairs - 1, dp_buf[:, (pairs - 1) * 384 :], turned)
    mixed_back(1)
    v_copy(0).start()
    send_mixed(1)
    passes((down, 2), (down + 2, 1), (down + 1, 2))
    mlp_out(0)
    passes((down + 3, 2), (into, 1))
    turn(dhb)
    product(outs, o_buf[t], usual)
    mlp_out(1)
    v_next(0)
    passes((mixes + 2, 0))
    v_next(1)
    passes((mixes, 0), (mixes + 1, 0), (outs, 0))
    finish_tokens(0)

    def down_out(i):
        order = turned if i == last else usual
        gdn_ref[:, i * TILE : (i + 1) * TILE] = finish(down + i, order)

    def into_out(i):
        order = turned if i == last else usual
        gin_ref[:, i * TILE : (i + 1) * TILE] = finish(into + i, order)

    def mix_out(p):
        value = finish(mixes + p, order_of[mixes + p])
        for kind in range(3):
            gqkv_ref[kind, :, p * 128 : (p + 1) * 128] = value[:, kind * 128 : (kind + 1) * 128]

    down_out(0)
    passes((down + 2, 2))
    down_out(1)
    passes((into + 1, 1), (into, 2), (into + 3, 2))
    down_out(2)
    down_out(3)
    passes((into + 2, 1), (into + 1, 2), (mixes + 2, 1))
    v_next(2)
    finish_block(0)
    into_out(0)
    passes((mixes, 1), (into + 2, 2))
    into_out(1)
    into_out(3)
    v_next(3)
    passes((mixes + 1, 1), (mixes, 2))
    into_out(2)
    passes((mixes + 2, 2), (outs, 1), (mixes + 1, 2))
    mix_out(0)
    finish_tokens(1)
    passes((outs, 2))
    mix_out(1)
    mix_out(2)
    v_next(4)
    vout[...] = vsum[BITS + 1]
    gout_ref[...] = finish(outs, usual)
    finish_block(1)

    for part in range(2):
        for step in range(4):
            wo_copy(step, part).wait_send()
    for s in range(seqs):
        for p in range(pairs):
            o_copy(s, p).wait_send()
        for i in range(wide):
            da_copy(s, i).wait_send()
            mlp_copy(s, i).wait_send()
        out_copy(0, block_h, s).wait()
        out_copy(1, gtok_h, s).wait()
    for n in range(blocks):
        for i in range(wide):
            dc_copy(n, i).wait_send()

    for piece in range(total):
        for k in range(BITS):
            g_copy(piece, k, order_of[piece]).wait_send()
    for k in range(BITS + 1):
        v_copy(k).wait_send()


def deliver(
    block_h,
    gtok_h,
    gqkv_h,
    gout_h,
    gin_h,
    gdn_h,
    small,
    block_o,
    gtok_o,
    gqkv_o,
    pair_o,
    gout_o,
    ob_o,
    gin_o,
    hb_o,
    gdn_o,
    mb_o,
    gain_o,
    shift_o,
    block_m,
    gtok_m,
    gqkv_m,
    gout_m,
    gin_m,
    gdn_m,
    sem,
):
    big = (
        (block_h, block_m, block_o),
        (gtok_h, gtok_m, gtok_o),
        (gqkv_h, gqkv_m, gqkv_o),
        (gout_h, gout_m, gout_o),
        (gin_h, gin_m, gin_o),
        (gdn_h, gdn_m, gdn_o),
    )
    first = [
        pltpu.make_async_copy(src, mid, sem.at[0, i]) for i, (src, mid, _) in enumerate(big)
    ]
    second = [
        pltpu.make_async_copy(mid, dst, sem.at[1, i]) for i, (_, mid, dst) in enumerate(big)
    ]
    for copy in first:
        copy.start()
    local, width, hidden = pair_o.shape[1], ob_o.shape[0], hb_o.shape[0]
    pair_o[0:1] = small[0:1, :local]
    pair_o[1:2] = small[0:1, local:]
    hb_o[...] = jnp.concatenate([small[1:2], small[2:3]], axis=1).reshape(hidden)
    ob_o[...] = small[3:4].reshape(width)
    mb_o[...] = small[4:5].reshape(width)
    gain_o[...] = small[5:7]
    shift_o[...] = small[7:9]
    for copy, after in zip(first, second):
        copy.wait()
        after.start()
    for copy in second:
        copy.wait()


def body(
    tokens,
    segment_ids,
    w_qkv,
    qv_bias,
    w_out,
    out_bias,
    w_in,
    hidden_bias,
    w_down,
    mlp_bias,
    ln_gain,
    ln_bias,
    cotangent,
    *,
    dp,
):
    seqs, length, width = tokens.shape
    count = seqs * length
    local = w_qkv.shape[2]
    hidden = w_in.shape[1]
    pairs = local // (2 * HEAD)
    stride = dp // WAYS
    strip = width // WAYS
    pieces = 2 * (hidden // TILE) + 1 + pairs
    hbm = pl.BlockSpec(memory_space=pl.ANY)
    vmem = pl.BlockSpec(memory_space=pltpu.VMEM)
    dma = pltpu.SemaphoreType.DMA
    wide = (count, width)
    big = (
        jax.ShapeDtypeStruct(wide, BF),
        jax.ShapeDtypeStruct(wide, BF),
        jax.ShapeDtypeStruct((3, strip, local), F32),
        jax.ShapeDtypeStruct((strip, local), F32),
        jax.ShapeDtypeStruct((strip, hidden), F32),
        jax.ShapeDtypeStruct((strip, hidden), F32),
    )
    outs = pl.pallas_call(
        functools.partial(kernel, stride),
        out_shape=big + (jax.ShapeDtypeStruct((16, width), F32),),
        in_specs=[hbm, vmem, hbm, vmem, hbm, vmem, hbm, vmem, hbm, vmem, vmem, vmem, hbm],
        out_specs=(hbm, hbm, vmem, vmem, vmem, vmem, vmem),
        scratch_shapes=[
            pltpu.VMEM(wide, BF),
            pltpu.VMEM(wide, BF),
            pltpu.VMEM((width, 3 * local), BF),
            pltpu.VMEM((2, width, local), BF),
            pltpu.VMEM((width, hidden), BF),
            pltpu.VMEM((width, hidden), BF),
            pltpu.VMEM((16, width), F32),
            pltpu.VMEM(wide, BF),
            pltpu.VMEM(wide, F32),
            pltpu.VMEM((count, 1), F32),
            pltpu.VMEM((count, 3 * local), BF),
            pltpu.VMEM((seqs * pairs, length, 2 * length), F32),
            pltpu.VMEM((2, count, local), BF),
            pltpu.VMEM(wide, F32),
            pltpu.VMEM(wide, F32),
            pltpu.VMEM((count, 1), F32),
            pltpu.VMEM(wide, BF),
            pltpu.VMEM((count, hidden), BF),
            pltpu.VMEM((count, hidden), BF),
            pltpu.VMEM(wide, BF),
            pltpu.VMEM(wide, BF),
            pltpu.VMEM(wide, BF),
            pltpu.VMEM(wide, BF),
            pltpu.VMEM(wide, BF),
            pltpu.VMEM(wide, BF),
            pltpu.VMEM((count, local), BF),
            pltpu.VMEM(wide, BF),
            pltpu.VMEM((count, 3 * local), BF),
            pltpu.VMEM((2, count, width), BF),
            pltpu.VMEM((width, count), BF),
            pltpu.VMEM((pieces, 2, 2, 2, 2, strip, TILE), BF),
            pltpu.VMEM((pieces, 2, 2, 2, strip, TILE), BF),
            pltpu.VMEM((pieces, 2, 2, strip, TILE), BF),
            pltpu.VMEM((pieces, 2, strip, TILE), BF),
            pltpu.VMEM((pieces, strip, TILE), BF),
            pltpu.VMEM((BITS + 2, 16, width), F32),
            pltpu.VMEM((BITS + 1, 16, width), F32),
            dma((5 + 3 * pairs,)),
            dma((4, 2)),
            dma((4, 2)),
            dma((seqs, pairs)),
            dma((seqs, pairs)),
            dma((3, count // BLOCK, width // 256)),
            dma((3, count // BLOCK, width // 256)),
            dma((pieces, BITS)),
            dma((pieces, BITS)),
            dma((BITS + 1,)),
            dma((BITS + 1,)),
            dma((2, seqs)),
        ],
        compiler_params=pltpu.CompilerParams(
            collective_id=0, has_side_effects=True, vmem_limit_bytes=60 * 2**20
        ),
        cost_estimate=pl.CostEstimate(
            flops=12 * 10**9, bytes_accessed=12 * 10**6, transcendentals=4 * 10**6
        ),
    )(
        tokens.reshape(wide),
        segment_ids,
        w_qkv.transpose(1, 0, 2),
        qv_bias,
        w_out,
        out_bias,
        w_in,
        hidden_bias,
        w_down,
        mlp_bias,
        ln_gain,
        ln_bias,
        cotangent.reshape(wide),
    )
    if stride > 1:
        groups = [[g * stride + i for i in range(stride)] for g in range(WAYS)]
        scatter = functools.partial(
            lax.psum_scatter, axis_name="dp", axis_index_groups=groups, tiled=True
        )
        outs = (
            *outs[:2],
            scatter(outs[2], scatter_dimension=1),
            *[scatter(v, scatter_dimension=0) for v in outs[3:6]],
            lax.psum(outs[6], "dp", axis_index_groups=groups),
        )
    shapes = [
        outs[0],
        outs[1],
        outs[2],
        jax.ShapeDtypeStruct((2, local), F32),
        outs[3],
        jax.ShapeDtypeStruct((width,), F32),
        outs[4],
        jax.ShapeDtypeStruct((hidden,), F32),
        outs[5],
        jax.ShapeDtypeStruct((width,), F32),
        jax.ShapeDtypeStruct((2, width), F32),
        jax.ShapeDtypeStruct((2, width), F32),
    ]
    placed = [hbm, hbm, hbm, vmem, hbm, vmem, hbm, vmem, hbm, vmem, vmem, vmem]
    done = pl.pallas_call(
        deliver,
        out_shape=tuple(jax.ShapeDtypeStruct(v.shape, v.dtype) for v in shapes),
        in_specs=[hbm] * 6 + [vmem],
        out_specs=tuple(placed),
        scratch_shapes=[pltpu.VMEM(v.shape, v.dtype) for v in outs[:6]] + [dma((2, 6))],
    )(*outs)
    return (
        done[0].reshape(tokens.shape),
        done[1].reshape(tokens.shape),
        done[2].transpose(1, 0, 2),
        *done[3:],
    )


def solution(mesh):
    return jax.shard_map(
        functools.partial(body, dp=mesh.shape["dp"]),
        mesh=mesh,
        in_specs=(
            P("dp", None, None),
            P("dp", None),
            P(None, None, "tensor"),
            P(None, "tensor"),
            P(None, "tensor"),
            P(),
            P(None, "tensor"),
            P("tensor"),
            P(None, "tensor"),
            P(),
            P(),
            P(),
            P("dp", None, None),
        ),
        out_specs=(
            P("dp", None, None),
            P("dp", None, None),
            P("dp", None, "tensor"),
            P(None, "tensor"),
            P("dp", "tensor"),
            P(),
            P("dp", "tensor"),
            P("tensor"),
            P("dp", "tensor"),
            P(),
            P(),
            P(),
        ),
        check_vma=False,
    )
```

```python
import functools

import jax
import jax.numpy as jnp
from jax import lax
from jax.experimental import pallas as pl
from jax.experimental.pallas import tpu as pltpu
from jax.sharding import PartitionSpec as P

MESH = pl.DeviceIdType.MESH
BF = jnp.bfloat16
F32 = jnp.float32
HEAD = 64
NORM_EPS = 1e-06
MASKED = -1000000000.0
BITS = 4
WAYS = 2**BITS
BLOCK = 256
CHUNK = 64
TILE = 384

PLAN = (
    ("prod", 6), ("prod", 1), ("prod", 7), ("pass", 6, 0), ("pass", 1, 0), ("prod", 2), ("prod", 3),
    ("prod", 4), ("pass", 3, 0), ("pass", 7, 0), ("pass", 2, 0), ("prod", 0), ("resid", 0),
    ("pass", 1, 1), ("pass", 0, 0), ("attb", 0, 2), ("pass", 4, 0), ("attb", 0, 0), ("pass", 6, 1),
    ("mlp", 0), ("prod", 5), ("pass", 5, 0), ("attb", 0, 1), ("resid", 1), ("attb", 1, 1),
    ("pass", 4, 1), ("pass", 7, 1), ("mixb", 0), ("pass", 1, 2), ("prod", 10), ("attb", 1, 0),
    ("prod", 9), ("pass", 2, 1), ("sda", 0), ("pass", 10, 0), ("pass", 9, 0), ("pass", 6, 2),
    ("attb", 1, 2), ("pass", 0, 1), ("mixb", 1), ("prod", 8), ("v", 0), ("pass", 4, 2),
    ("pass", 8, 0), ("pass", 7, 2), ("pass", 3, 1), ("pass", 2, 2), ("fin", 1), ("prod", 11),
    ("pass", 9, 1), ("pass", 10, 1), ("sda", 1), ("pass", 0, 2), ("pass", 11, 0), ("pass", 5, 1),
    ("pass", 3, 2), ("ft", 0), ("v", 1), ("pass", 8, 1), ("pass", 10, 2), ("fin", 2), ("fb", 0),
    ("pass", 5, 2), ("pass", 9, 2), ("v", 2), ("fin", 6), ("fin", 7), ("mlp", 1), ("pass", 11, 1),
    ("fin", 4), ("pass", 8, 2), ("v", 3), ("pass", 11, 2), ("fin", 3), ("v", 4), ("fin", 5),
    ("ft", 1), ("fin", 9), ("fin", 11), ("fin", 0), ("fin", 8), ("v", 5), ("fin", 10), ("fb", 1),
)
HALVINGS = (
    (0, 2, 1, 3),
    (0, 1, 2, 3),
    (0, 1, 2, 3),
    (0, 2, 1, 3),
    (0, 1, 2, 3),
    (0, 1, 2, 3),
    (0, 2, 1, 3),
    (0, 2, 1, 3),
    (0, 1, 2, 3),
    (0, 2, 1, 3),
    (0, 1, 2, 3),
    (0, 1, 2, 3),
)

NN = ((1,), (0,))
NT = ((1,), (1,))
TN = ((0,), (0,))


def dot(a, b, dims):
    return lax.dot_general(a, b, (dims, ((), ())), preferred_element_type=F32)


def loop(count, step):
    def run(i, carry):
        step(i)
        return carry

    lax.fori_loop(0, count, run, 0)


def each(count, step):
    for i in range(count):
        step(i)


def rows(i, size):
    if isinstance(i, int):
        return slice(i * size, (i + 1) * size)
    return pl.ds(pl.multiple_of(i * size, size), size)


cols = rows


def kernel(
    stride,
    tok_h,
    seg_ref,
    wqkv_h,
    qvb_ref,
    wout_h,
    ob_ref,
    win_h,
    hb_ref,
    wdn_h,
    mb_ref,
    gain_ref,
    shift_ref,
    dy_h,
    block_ref,
    gtok_ref,
    gqkv_ref,
    gout_ref,
    gin_ref,
    gdn_ref,
    vout,
    tok,
    dy,
    wq,
    wo,
    win,
    wdn,
    vin,
    a_buf,
    xh1,
    r1,
    qkv,
    p_buf,
    o_buf,
    h_buf,
    xh2,
    r2,
    c_buf,
    g_buf,
    du_buf,
    dc_snd,
    dc_rcv,
    mlp_snd,
    mlp_rcv,
    da_snd,
    da_rcv,
    do_buf,
    dhb,
    dp_buf,
    grads,
    r0_buf,
    r1_buf,
    r2_buf,
    r3_buf,
    vsum,
    vrcv,
    in_sem,
    wo_send,
    wo_recv,
    o_send,
    o_recv,
    x_send,
    x_recv,
    g_send,
    g_recv,
    v_send,
    v_recv,
):
    d = lax.axis_index("dp")
    t = lax.axis_index("tensor")
    group = d // stride
    bit = [lax.rem(group // (2**b), 2) for b in range(BITS)]
    mate = [d + (1 - 2 * bit[b]) * (2**b) * stride for b in range(BITS)]
    count, width = tok.shape
    seqs = seg_ref.shape[0]
    length = count // seqs
    local = wo.shape[2]
    pairs = local // (2 * HEAD)
    hidden = win.shape[1]
    scale = HEAD ** (-0.5)
    blocks = count // BLOCK
    vacc = vsum.at[0]

    barrier = pltpu.get_barrier_semaphore()
    pl.semaphore_signal(barrier, inc=1, device_id=(d, 1 - t), device_id_type=MESH)
    for b in range(BITS):
        pl.semaphore_signal(barrier, inc=1, device_id=(mate[b], t), device_id_type=MESH)

    loads = []

    def load(src, dst):
        copy = pltpu.make_async_copy(src, dst, in_sem.at[len(loads)])
        copy.start()
        loads.append(copy)
        return copy

    tok_load = load(tok_h, tok)
    wq_loads = [
        load(
            wqkv_h.at[kind, :, p * 128 : (p + 1) * 128],
            wq.at[:, p * 384 + kind * 128 : p * 384 + (kind + 1) * 128],
        )
        for p in range(pairs)
        for kind in range(3)
    ]
    dy_load = load(dy_h, dy)
    wo_load = load(wout_h, wo.at[t])
    win_load = load(win_h, win)
    wdn_load = load(wdn_h, wdn)

    def across(src, dst, send, recv):
        return pltpu.make_async_remote_copy(
            src_ref=src,
            dst_ref=dst,
            send_sem=send,
            recv_sem=recv,
            device_id=(d, 1 - t),
            device_id_type=MESH,
        )

    def toward(b, src, dst, send, recv):
        return pltpu.make_async_remote_copy(
            src_ref=src,
            dst_ref=dst,
            send_sem=send,
            recv_sem=recv,
            device_id=(mate[b], t),
            device_id_type=MESH,
        )

    slab = width // 8

    def wo_rows(turned, part):
        first = bit[0]
        second = 1 - bit[1] if turned else bit[1]
        return rows((2 * second + first) * 2 + part, slab)

    def wo_copy(step, part):
        sems = wo_send.at[step, part], wo_recv.at[step, part]
        if step == 0:
            here = wo_rows(False, part)
            return across(wout_h.at[here], wo.at[t, here], *sems)
        here = wo_rows(step == 3, part)
        return toward(1 if step == 2 else 0, wo.at[1 - t, here], wo.at[1 - t, here], *sems)

    def wo_share(part):
        wo_copy(0, part).wait_recv()
        wo_copy(2, part).start()
        wo_copy(1, part).start()

    def wo_forward(part):
        wo_copy(2, part).wait_recv()
        wo_copy(3, part).start()

    def o_copy(s, p):
        here = rows(s, length)
        place = o_buf.at[t, here, cols(p, 128)]
        return across(place, place, o_send.at[s, p], o_recv.at[s, p])

    def dc_copy(n, i):
        here = rows(n, BLOCK), cols(i, 256)
        return across(
            dc_snd.at[here], dc_rcv.at[here], x_send.at[0, n, i], x_recv.at[0, n, i]
        )

    def da_copy(s, i):
        here = rows(s, length), cols(i, 256)
        return across(
            da_snd.at[here], da_rcv.at[here], x_send.at[1, s, i], x_recv.at[1, s, i]
        )

    def mlp_copy(s, i):
        here = rows(s, length), cols(i, 256)
        return across(
            mlp_snd.at[here], mlp_rcv.at[here], x_send.at[2, s, i], x_recv.at[2, s, i]
        )

    wide = width // 256

    vacc[...] = jnp.zeros(vacc.shape, F32)
    vin[0:2] = gain_ref[...].astype(F32)
    vin[2:4] = shift_ref[...].astype(F32)
    vin[4:5] = ob_ref[...].astype(F32).reshape(1, width)
    vin[5:6] = mb_ref[...].astype(F32).reshape(1, width)
    line = hb_ref[...].astype(F32).reshape(1, hidden)
    vin[6:7] = line[:, :width]
    vin[7:8] = line[:, width:]
    vin[8:9, :local] = qvb_ref[0:1].astype(F32)
    vin[8:9, local:] = qvb_ref[1:2].astype(F32)

    lane = lax.broadcasted_iota(jnp.int32, (1, 128), 1)
    low_half = lane < HEAD

    def stacked(value):
        zero = jnp.zeros_like(value)
        return jnp.concatenate(
            [jnp.where(low_half, value, zero), jnp.where(low_half, zero, value)], axis=0
        )

    def normalize(value):
        mean = jnp.sum(value, axis=-1, keepdims=True) * (1.0 / width)
        center = value - mean
        spread = jnp.sum(center * center, axis=-1, keepdims=True) * (1.0 / width)
        scale_back = lax.rsqrt(spread + NORM_EPS)
        return center * scale_back, scale_back

    def norm_back(grad, normed, scale_back, gain):
        inner = grad * gain
        mean_one = jnp.sum(inner, axis=-1, keepdims=True) * (1.0 / width)
        mean_two = jnp.sum(inner * normed, axis=-1, keepdims=True) * (1.0 / width)
        return scale_back * (inner - mean_one - normed * mean_two)

    def same_image(s):
        ids = seg_ref[s : s + 1].astype(F32)
        down = jnp.broadcast_to(ids, (128, length)).T
        return jnp.concatenate(
            [down == ids[:, i * 128 : (i + 1) * 128] for i in range(length // 128)], axis=1
        )

    def norm_one(s):
        def step(i):
            here = rows(s * (length // CHUNK) + i, CHUNK)
            normed, scale_back = normalize(tok[here].astype(F32))
            xh1[here] = normed
            r1[here] = scale_back
            a_buf[here] = (normed * vin[0:1] + vin[2:3]).astype(BF)

        each(length // CHUNK, step)

    def attention(s):
        seq = rows(s, length)
        allowed = same_image(s)

        def pair_step(p):
            bias = jnp.concatenate(
                [
                    vin[8:9, cols(p, 128)],
                    jnp.zeros((1, 128), F32),
                    vin[8:9, cols(pairs + p, 128)],
                ],
                axis=1,
            )
            mixed = (dot(a_buf[seq], wq[:, cols(p, 384)], NN) + bias).astype(BF)
            qkv[seq, cols(p, 384)] = mixed
            scores = dot(mixed[:, :128], stacked(mixed[:, 128:256]), NT) * scale
            soft = []
            for e in range(2):
                one = jnp.where(allowed, scores[:, e * length : (e + 1) * length], MASKED)
                expo = jnp.exp(one - jnp.max(one, axis=-1, keepdims=True))
                soft.append(expo * (1.0 / jnp.sum(expo, axis=-1, keepdims=True)))
            both = jnp.concatenate(soft, axis=1)
            p_buf[s * pairs + p] = both
            o_buf[t, seq, cols(p, 128)] = dot(
                both.astype(BF), stacked(mixed[:, 256:]), NN
            ).astype(BF)
            o_copy(s, p).start()

        each(pairs, pair_step)

    tok_load.wait()
    norm_one(0)
    norm_one(1)
    pl.semaphore_wait(barrier, BITS + 1)
    wo_copy(0, 0).start()
    wo_copy(0, 1).start()
    for copy in wq_loads:
        copy.wait()
    attention(0)
    wo_share(0)
    wo_share(1)
    attention(1)

    strip = width // WAYS
    received = [r0_buf, r1_buf, r2_buf, r3_buf]

    def product(piece, left, right, order):
        full = dot(left[...], right, TN)
        for k in range(WAYS):
            b = [(k >> i) & 1 for i in order]
            grads[piece, b[0], b[1], b[2], b[3]] = full[k * strip : (k + 1) * strip].astype(BF)
        g_copy(piece, 0, order).start()

    def own(piece, depth, order):
        return (piece,) + tuple(bit[b] for b in order[:depth])

    def g_copy(piece, k, order):
        return toward(
            order[k],
            grads.at[own(piece, k, order) + (1 - bit[order[k]],)],
            received[k].at[piece],
            g_send.at[piece, k],
            g_recv.at[piece, k],
        )

    def pass_on(piece, k, order):
        g_copy(piece, k, order).wait_recv()
        here = own(piece, k + 1, order)
        grads[here] = (grads[here].astype(F32) + received[k][piece].astype(F32)).astype(BF)
        g_copy(piece, k + 1, order).start()

    def finish(piece, order):
        g_copy(piece, 3, order).wait_recv()
        return grads[own(piece, 4, order)].astype(F32) + received[3][piece].astype(F32)

    hidden_pieces = hidden // TILE
    down, into, outs, mixes = 0, hidden_pieces, 2 * hidden_pieces, 2 * hidden_pieces + 1
    total = mixes + pairs

    dy_load.wait()
    vacc[4:5] += jnp.sum(dy[...].astype(F32), axis=0, keepdims=True)
    wo_load.wait()
    win_load.wait()
    wdn_load.wait()
    for part in range(2):
        wo_forward(part)
    for part in range(2):
        wo_copy(1, part).wait_recv()
        wo_copy(3, part).wait_recv()

    per = length // BLOCK

    def middle(n):
        here = rows(n, BLOCK)

        @pl.when(lax.rem(n, per) == 0)
        def _():
            for p in range(pairs):
                o_copy(n // per, p).wait_recv()

        h_buf[here] = dot(o_buf[0, here], wo[0], NT) + dot(o_buf[1, here], wo[1], NT)

        def norm_step(i):
            few = rows(n * (BLOCK // CHUNK) + i, CHUNK)
            resid = h_buf[few] + vin[4:5] + tok[few].astype(F32)
            h_buf[few] = resid
            normed, scale_back = normalize(resid)
            xh2[few] = normed
            r2[few] = scale_back
            c_buf[few] = (normed * vin[1:2] + vin[3:4]).astype(BF)

        each(BLOCK // CHUNK, norm_step)

        for m in range(hidden // width):

            def hidden_step(i, m=m):
                there = cols(i, 256)
                part = cols(m * wide + i, 256)
                pre = dot(c_buf[here], win[:, part], NN) + vin[6 + m : 7 + m, there]
                back = dot(dy[here], wdn[:, part], NN)
                phi = 0.5 + 0.5 * lax.erf(pre * 0.7071067811865476)
                g_buf[here, part] = (pre * phi).astype(BF)
                slope = phi + pre * (jnp.exp(-0.5 * pre * pre) * 0.3989422804014327)
                low = (back * slope).astype(BF)
                du_buf[here, part] = low
                vacc[1 + m : 2 + m, there] += jnp.sum(low.astype(F32), axis=0, keepdims=True)

            each(wide, hidden_step)

        def back_step(i):
            there = cols(i, 256)
            grad = dot(du_buf[here], win[rows(i, 256)], NT)
            dc_snd[here, there] = grad.astype(BF)
            dc_copy(n, i).start()
            vacc[6:7, there] += jnp.sum(grad * xh2[here, there], axis=0, keepdims=True)
            vacc[8:9, there] += jnp.sum(grad, axis=0, keepdims=True)

        each(wide, back_step)

    loop(blocks, middle)

    def mlp_out(s):
        seq = rows(s, length)

        def step(i):
            mlp_snd[seq, cols(i, 256)] = dot(g_buf[seq], wdn[rows(i, 256)], NT).astype(BF)
            mlp_copy(s, i).start()

        each(wide, step)

    def resid_back(s):
        seq = rows(s, length)
        for n in range(s * per, (s + 1) * per):
            for i in range(wide):
                dc_copy(n, i).wait_recv()

        def step(i):
            here = rows(s * (length // CHUNK) + i, CHUNK)
            grad = dc_snd[here].astype(F32) + dc_rcv[here].astype(F32)
            full = dy[here].astype(F32) + norm_back(grad, xh2[here], r2[here], vin[1:2])
            xh2[here] = full
            dhb[here] = full.astype(BF)
            vacc[3:4] += jnp.sum(full, axis=0, keepdims=True)

        each(length // CHUNK, step)
        do_buf[seq] = dot(dhb[seq], wo[t], NN).astype(BF)

    def attention_back(s, p):
        seq = rows(s, length)
        mixed = qkv[seq, cols(p, 384)]
        query, keys = mixed[:, :128], stacked(mixed[:, 128:256])
        grad_o = do_buf[seq, cols(p, 128)]
        soft = p_buf[s * pairs + p]
        grad_soft = dot(grad_o, stacked(mixed[:, 256:]), NT)
        parts = []
        for e in range(2):
            one, two = (v[:, e * length : (e + 1) * length] for v in (soft, grad_soft))
            delta = jnp.sum(one * two, axis=-1, keepdims=True)
            parts.append((one * (two - delta)).astype(BF))
        grad_scores = jnp.concatenate(parts, axis=1)
        grad_query = dot(grad_scores, keys, NN) * scale
        grad_keys = dot(grad_scores, query, TN) * scale
        grad_keys = jnp.where(low_half, grad_keys[:length], grad_keys[length:])
        grad_values = dot(soft.astype(BF), grad_o, TN)
        grad_values = jnp.where(low_half, grad_values[:length], grad_values[length:])
        low = [v.astype(BF) for v in (grad_query, grad_keys, grad_values)]
        dp_buf[seq, cols(p, 384)] = jnp.concatenate(low, axis=1)
        vacc[0:1, cols(p, 128)] += jnp.sum(low[0].astype(F32), axis=0, keepdims=True)
        vacc[0:1, cols(pairs + p, 128)] += jnp.sum(low[2].astype(F32), axis=0, keepdims=True)

    def mixed_back(s):
        seq = rows(s, length)

        def step(i):
            here = cols(i, 256)
            grad = dot(dp_buf[seq], wq[rows(i, 256)], NT)
            da_snd[seq, here] = grad.astype(BF)
            vacc[5:6, here] += jnp.sum(grad * xh1[seq, here], axis=0, keepdims=True)
            vacc[7:8, here] += jnp.sum(grad, axis=0, keepdims=True)

        each(wide, step)

    def send_mixed(s):
        for i in range(wide):
            da_copy(s, i).start()

    def finish_block(s):
        seq = rows(s, length)

        def step(i):
            mlp_copy(s, i).wait_recv()
            here = seq, cols(i, 256)
            added = mlp_snd[here].astype(F32) + mlp_rcv[here].astype(F32)
            block_ref[seq, cols(i, 256)] = (h_buf[here] + (added + vin[5:6, cols(i, 256)])).astype(BF)

        each(wide, step)

    def finish_tokens(s):
        for i in range(wide):
            da_copy(s, i).wait_recv()

        def step(i):
            here = rows(s * (length // CHUNK) + i, CHUNK)
            grad = da_snd[here].astype(F32) + da_rcv[here].astype(F32)
            full = xh2[here] + norm_back(grad, xh1[here], r1[here], vin[0:1])
            gtok_ref[here] = full.astype(BF)

        each(length // CHUNK, step)

    def v_copy(k):
        sems = v_send.at[k], v_recv.at[k]
        if k == 0:
            return across(vsum.at[0], vrcv.at[0], *sems)
        return toward(k - 1, vsum.at[k], vrcv.at[k], *sems)

    def v_next(k):
        v_copy(k).wait_recv()
        if k == 0:
            line = lax.broadcasted_iota(jnp.int32, vacc.shape, 0)
            norms = (line >= 5) & (line < 9)
            vsum[1] = jnp.where(norms, vsum[0] + vrcv[0], vsum[0])
        else:
            vsum[k + 1] = vsum[k] + vrcv[k]
        if k < BITS:
            v_copy(k + 1).start()

    def prod(piece):
        order = HALVINGS[piece]
        if piece < into:
            product(piece, dy, g_buf[:, cols(piece, TILE)], order)
        elif piece < outs:
            product(piece, c_buf, du_buf[:, cols(piece - into, TILE)], order)
        elif piece < mixes:
            product(piece, dhb, o_buf[t], order)
        else:
            product(piece, a_buf, dp_buf[:, cols(piece - mixes, 384)], order)

    def fin(piece):
        value = finish(piece, HALVINGS[piece])
        if piece < into:
            gdn_ref[:, cols(piece, TILE)] = value
        elif piece < outs:
            gin_ref[:, cols(piece - into, TILE)] = value
        elif piece < mixes:
            gout_ref[...] = value
        else:
            for kind in range(3):
                gqkv_ref[kind, :, cols(piece - mixes, 128)] = value[:, cols(kind, 128)]

    def small(k):
        if k == 0:
            v_copy(0).start()
        else:
            v_next(k - 1)
        if k == BITS + 1:
            vout[...] = vsum[k]

    steps = {
        "prod": prod,
        "pass": lambda piece, k: pass_on(piece, k, HALVINGS[piece]),
        "fin": fin,
        "resid": resid_back,
        "attb": attention_back,
        "mixb": mixed_back,
        "sda": send_mixed,
        "mlp": mlp_out,
        "fb": finish_block,
        "ft": finish_tokens,
        "v": small,
    }
    for name, *which in PLAN:
        steps[name](*which)

    for part in range(2):
        for step in range(4):
            wo_copy(step, part).wait_send()
    for s in range(seqs):
        for p in range(pairs):
            o_copy(s, p).wait_send()
        for i in range(wide):
            da_copy(s, i).wait_send()
            mlp_copy(s, i).wait_send()
    for n in range(blocks):
        for i in range(wide):
            dc_copy(n, i).wait_send()

    for piece in range(total):
        for k in range(BITS):
            g_copy(piece, k, HALVINGS[piece]).wait_send()
    for k in range(BITS + 1):
        v_copy(k).wait_send()


def deliver(
    block_v,
    gtok_v,
    gqkv_v,
    gout_v,
    gin_v,
    gdn_v,
    small,
    block_o,
    gtok_o,
    gqkv_o,
    pair_o,
    gout_o,
    ob_o,
    gin_o,
    hb_o,
    gdn_o,
    mb_o,
    gain_o,
    shift_o,
    sem,
):
    big = (
        (block_v, block_o),
        (gtok_v, gtok_o),
        (gqkv_v, gqkv_o),
        (gout_v, gout_o),
        (gin_v, gin_o),
        (gdn_v, gdn_o),
    )
    copies = [pltpu.make_async_copy(src, dst, sem.at[i]) for i, (src, dst) in enumerate(big)]
    for copy in copies:
        copy.start()
    local, width, hidden = pair_o.shape[1], ob_o.shape[0], hb_o.shape[0]
    pair_o[0:1] = small[0:1, :local]
    pair_o[1:2] = small[0:1, local:]
    hb_o[...] = jnp.concatenate([small[1:2], small[2:3]], axis=1).reshape(hidden)
    ob_o[...] = small[3:4].reshape(width)
    mb_o[...] = small[4:5].reshape(width)
    gain_o[...] = small[5:7]
    shift_o[...] = small[7:9]
    for copy in copies:
        copy.wait()


def body(
    tokens,
    segment_ids,
    w_qkv,
    qv_bias,
    w_out,
    out_bias,
    w_in,
    hidden_bias,
    w_down,
    mlp_bias,
    ln_gain,
    ln_bias,
    cotangent,
    *,
    dp,
):
    seqs, length, width = tokens.shape
    count = seqs * length
    local = w_qkv.shape[2]
    hidden = w_in.shape[1]
    pairs = local // (2 * HEAD)
    stride = dp // WAYS
    strip = width // WAYS
    pieces = 2 * (hidden // TILE) + 1 + pairs
    hbm = pl.BlockSpec(memory_space=pl.ANY)
    vmem = pl.BlockSpec(memory_space=pltpu.VMEM)
    dma = pltpu.SemaphoreType.DMA
    wide = (count, width)
    big = (
        pltpu.VMEM(wide, BF),
        pltpu.VMEM(wide, BF),
        pltpu.VMEM((3, strip, local), F32),
        pltpu.VMEM((strip, local), F32),
        pltpu.VMEM((strip, hidden), F32),
        pltpu.VMEM((strip, hidden), F32),
    )
    outs = pl.pallas_call(
        functools.partial(kernel, stride),
        out_shape=big + (pltpu.VMEM((16, width), F32),),
        in_specs=[hbm, vmem, hbm, vmem, hbm, vmem, hbm, vmem, hbm, vmem, vmem, vmem, hbm],
        out_specs=(vmem,) * 7,
        scratch_shapes=[
            pltpu.VMEM(wide, BF),
            pltpu.VMEM(wide, BF),
            pltpu.VMEM((width, 3 * local), BF),
            pltpu.VMEM((2, width, local), BF),
            pltpu.VMEM((width, hidden), BF),
            pltpu.VMEM((width, hidden), BF),
            pltpu.VMEM((16, width), F32),
            pltpu.VMEM(wide, BF),
            pltpu.VMEM(wide, F32),
            pltpu.VMEM((count, 1), F32),
            pltpu.VMEM((count, 3 * local), BF),
            pltpu.VMEM((seqs * pairs, length, 2 * length), F32),
            pltpu.VMEM((2, count, local), BF),
            pltpu.VMEM(wide, F32),
            pltpu.VMEM(wide, F32),
            pltpu.VMEM((count, 1), F32),
            pltpu.VMEM(wide, BF),
            pltpu.VMEM((count, hidden), BF),
            pltpu.VMEM((count, hidden), BF),
            pltpu.VMEM(wide, BF),
            pltpu.VMEM(wide, BF),
            pltpu.VMEM(wide, BF),
            pltpu.VMEM(wide, BF),
            pltpu.VMEM(wide, BF),
            pltpu.VMEM(wide, BF),
            pltpu.VMEM((count, local), BF),
            pltpu.VMEM(wide, BF),
            pltpu.VMEM((count, 3 * local), BF),
            pltpu.VMEM((pieces, 2, 2, 2, 2, strip, TILE), BF),
            pltpu.VMEM((pieces, 2, 2, 2, strip, TILE), BF),
            pltpu.VMEM((pieces, 2, 2, strip, TILE), BF),
            pltpu.VMEM((pieces, 2, strip, TILE), BF),
            pltpu.VMEM((pieces, strip, TILE), BF),
            pltpu.VMEM((BITS + 2, 16, width), F32),
            pltpu.VMEM((BITS + 1, 16, width), F32),
            dma((5 + 3 * pairs,)),
            dma((4, 2)),
            dma((4, 2)),
            dma((seqs, pairs)),
            dma((seqs, pairs)),
            dma((3, count // BLOCK, width // 256)),
            dma((3, count // BLOCK, width // 256)),
            dma((pieces, BITS)),
            dma((pieces, BITS)),
            dma((BITS + 1,)),
            dma((BITS + 1,)),
        ],
        compiler_params=pltpu.CompilerParams(
            collective_id=0, has_side_effects=True, vmem_limit_bytes=56 * 2**20
        ),
        cost_estimate=pl.CostEstimate(
            flops=12 * 10**9, bytes_accessed=12 * 10**6, transcendentals=4 * 10**6
        ),
    )(
        tokens.reshape(wide),
        segment_ids,
        w_qkv.transpose(1, 0, 2),
        qv_bias,
        w_out,
        out_bias,
        w_in,
        hidden_bias,
        w_down,
        mlp_bias,
        ln_gain,
        ln_bias,
        cotangent.reshape(wide),
    )
    if stride > 1:
        groups = [[g * stride + i for i in range(stride)] for g in range(WAYS)]
        scatter = functools.partial(
            lax.psum_scatter, axis_name="dp", axis_index_groups=groups, tiled=True
        )
        outs = (
            *outs[:2],
            scatter(outs[2], scatter_dimension=1),
            *[scatter(v, scatter_dimension=0) for v in outs[3:6]],
            lax.psum(outs[6], "dp", axis_index_groups=groups),
        )
    shapes = [
        outs[0],
        outs[1],
        outs[2],
        jax.ShapeDtypeStruct((2, local), F32),
        outs[3],
        jax.ShapeDtypeStruct((width,), F32),
        outs[4],
        jax.ShapeDtypeStruct((hidden,), F32),
        outs[5],
        jax.ShapeDtypeStruct((width,), F32),
        jax.ShapeDtypeStruct((2, width), F32),
        jax.ShapeDtypeStruct((2, width), F32),
    ]
    placed = [hbm, hbm, hbm, vmem, hbm, vmem, hbm, vmem, hbm, vmem, vmem, vmem]
    done = pl.pallas_call(
        deliver,
        out_shape=tuple(jax.ShapeDtypeStruct(v.shape, v.dtype) for v in shapes),
        in_specs=[vmem] * 7,
        out_specs=tuple(placed),
        scratch_shapes=[dma((6,))],
    )(*[pltpu.with_memory_space_constraint(v, pltpu.VMEM) for v in outs])
    return (
        done[0].reshape(tokens.shape),
        done[1].reshape(tokens.shape),
        done[2].transpose(1, 0, 2),
        *done[3:],
    )


def solution(mesh):
    return jax.shard_map(
        functools.partial(body, dp=mesh.shape["dp"]),
        mesh=mesh,
        in_specs=(
            P("dp", None, None),
            P("dp", None),
            P(None, None, "tensor"),
            P(None, "tensor"),
            P(None, "tensor"),
            P(),
            P(None, "tensor"),
            P("tensor"),
            P(None, "tensor"),
            P(),
            P(),
            P(),
            P("dp", None, None),
        ),
        out_specs=(
            P("dp", None, None),
            P("dp", None, None),
            P("dp", None, "tensor"),
            P(None, "tensor"),
            P("dp", "tensor"),
            P(),
            P("dp", "tensor"),
            P("tensor"),
            P("dp", "tensor"),
            P(),
            P(),
            P(),
        ),
        check_vma=False,
    )
```

```python
import functools

import jax
import jax.numpy as jnp
from jax import lax
from jax.experimental import pallas as pl
from jax.experimental.pallas import tpu as pltpu
from jax.sharding import PartitionSpec as P

MESH = pl.DeviceIdType.MESH
BF = jnp.bfloat16
F32 = jnp.float32
HEAD = 64
NORM_EPS = 1e-06
MASKED = -1000000000.0
BITS = 4
WAYS = 2**BITS
BLOCK = 256
CHUNK = 64
TILE = 384

PLAN = (
    ("prod", 0), ("prod", 7), ("mb", 1), ("pass", 0, 0), ("prod", 4), ("pass", 7, 0), ("prod", 2),
    ("prod", 1), ("prod", 3), ("resid", 0), ("pass", 2, 0), ("pass", 3, 0), ("pass", 4, 0),
    ("pass", 1, 0), ("resid", 1), ("prod", 8), ("pass", 0, 1), ("prod", 12), ("pass", 8, 0),
    ("attb", 0, 1), ("mlp", 1), ("pass", 7, 1), ("attb", 1, 0), ("prod", 5), ("pass", 2, 1),
    ("pass", 3, 1), ("attb", 0, 0), ("attb", 0, 2), ("pass", 5, 0), ("attb", 1, 2), ("prod", 11),
    ("mixb", 0), ("pass", 1, 1), ("pass", 12, 0), ("pass", 0, 2), ("attb", 1, 1), ("mixb", 1),
    ("prod", 6), ("v", 0), ("pass", 2, 2), ("sda", 0), ("pass", 8, 1), ("pass", 3, 2),
    ("pass", 11, 0), ("prod", 9), ("prod", 10), ("pass", 5, 1), ("mlp", 0), ("pass", 6, 0),
    ("fb", 1), ("v", 1), ("v", 2), ("pass", 1, 2), ("pass", 12, 1), ("pass", 11, 1), ("sda", 1),
    ("pass", 8, 2), ("pass", 5, 2), ("pass", 9, 0), ("pass", 7, 2), ("v", 3), ("pass", 12, 2),
    ("pass", 10, 0), ("pass", 6, 1), ("pass", 11, 2), ("v", 4), ("ft", 0), ("fin", 3),
    ("pass", 4, 1), ("pass", 9, 1), ("pass", 6, 2), ("fo",), ("pass", 10, 1), ("fin", 0), ("ft", 1),
    ("pass", 4, 2), ("pass", 9, 2), ("fin", 5), ("fin", 1), ("pass", 10, 2), ("fb", 0), ("fin", 7),
    ("fin", 4), ("fin", 2), ("fin", 9), ("fin", 6), ("v", 5), ("foe",), ("fin", 11), ("fin", 10),
    ("gt", 0), ("gt", 1),
)
HALVINGS = (
    (0, 1, 2, 3),
    (0, 1, 2, 3),
    (0, 1, 2, 3),
    (0, 1, 2, 3),
    (0, 2, 1, 3),
    (0, 1, 2, 3),
    (0, 1, 2, 3),
    (0, 2, 1, 3),
    (0, 2, 1, 3),
    (0, 1, 2, 3),
    (0, 1, 2, 3),
    (0, 2, 1, 3),
    (0, 1, 2, 3),
)

NN = ((1,), (0,))
NT = ((1,), (1,))
TN = ((0,), (0,))


def dot(a, b, dims):
    return lax.dot_general(a, b, (dims, ((), ())), preferred_element_type=F32)


def each(count, step):
    for i in range(count):
        step(i)


def rows(i, size):
    if isinstance(i, int):
        return slice(i * size, (i + 1) * size)
    return pl.ds(pl.multiple_of(i * size, size), size)


cols = rows


def kernel(
    stride,
    tok_h,
    seg_ref,
    wqkv_h,
    qvb_ref,
    wout_h,
    ob_ref,
    win_h,
    hb_ref,
    wdn_h,
    mb_ref,
    gain_ref,
    shift_ref,
    dy_h,
    block_ref,
    gtok_ref,
    gqkv_ref,
    gout_ref,
    gin_ref,
    gdn_ref,
    vout,
    tok,
    dy,
    wq,
    wo,
    win,
    wdn,
    vin,
    a_buf,
    xh1,
    r1,
    qkv,
    p_buf,
    o_buf,
    h_buf,
    xh2,
    r2,
    c_buf,
    back_buf,
    g_buf,
    du_buf,
    dc_snd,
    dc_rcv,
    mlp_snd,
    mlp_rcv,
    da_snd,
    da_rcv,
    do_buf,
    do_snd,
    dhb,
    fo_buf,
    dp_buf,
    grads,
    r0_buf,
    r1_buf,
    r2_buf,
    r3_buf,
    vsum,
    vrcv,
    in_sem,
    wo_send,
    wo_recv,
    o_send,
    o_recv,
    x_send,
    x_recv,
    y_send,
    y_recv,
    g_send,
    g_recv,
    v_send,
    v_recv,
):
    d = lax.axis_index("dp")
    t = lax.axis_index("tensor")
    group = d // stride
    bit = [lax.rem(group // (2**b), 2) for b in range(BITS)]
    mate = [d + (1 - 2 * bit[b]) * (2**b) * stride for b in range(BITS)]
    count, width = tok.shape
    seqs = seg_ref.shape[0]
    length = count // seqs
    local = wo.shape[2]
    pairs = local // (2 * HEAD)
    hidden = win.shape[1]
    scale = HEAD ** (-0.5)
    vacc = vsum.at[0]

    barrier = pltpu.get_barrier_semaphore()
    pl.semaphore_signal(barrier, inc=1, device_id=(d, 1 - t), device_id_type=MESH)
    for b in range(BITS):
        pl.semaphore_signal(barrier, inc=1, device_id=(mate[b], t), device_id_type=MESH)

    loads = []

    def load(src, dst):
        copy = pltpu.make_async_copy(src, dst, in_sem.at[len(loads)])
        copy.start()
        loads.append(copy)
        return copy

    tok_load = load(tok_h, tok)
    wq_loads = [
        load(
            wqkv_h.at[kind, :, p * 128 : (p + 1) * 128],
            wq.at[:, p * 384 + kind * 128 : p * 384 + (kind + 1) * 128],
        )
        for p in range(pairs)
        for kind in range(3)
    ]
    dy_load = load(dy_h, dy)
    wo_load = load(wout_h, wo.at[t])
    win_load = load(win_h, win)
    wdn_load = load(wdn_h, wdn)

    def across(src, dst, send, recv):
        return pltpu.make_async_remote_copy(
            src_ref=src,
            dst_ref=dst,
            send_sem=send,
            recv_sem=recv,
            device_id=(d, 1 - t),
            device_id_type=MESH,
        )

    def toward(b, src, dst, send, recv):
        return pltpu.make_async_remote_copy(
            src_ref=src,
            dst_ref=dst,
            send_sem=send,
            recv_sem=recv,
            device_id=(mate[b], t),
            device_id_type=MESH,
        )

    slab = width // 8

    def wo_rows(turned, part):
        first = bit[0]
        second = 1 - bit[1] if turned else bit[1]
        return rows((2 * second + first) * 2 + part, slab)

    def wo_copy(step, part):
        sems = wo_send.at[step, part], wo_recv.at[step, part]
        if step == 0:
            here = wo_rows(False, part)
            return across(wout_h.at[here], wo.at[t, here], *sems)
        here = wo_rows(step == 3, part)
        return toward(1 if step == 2 else 0, wo.at[1 - t, here], wo.at[1 - t, here], *sems)

    def wo_share(part):
        wo_copy(0, part).wait_recv()
        wo_copy(2, part).start()
        wo_copy(1, part).start()

    def wo_forward(part):
        wo_copy(2, part).wait_recv()
        wo_copy(3, part).start()

    def o_copy(s, p):
        here = rows(s, length)
        place = o_buf.at[t, here, cols(p, 128)]
        return across(place, place, o_send.at[s, p], o_recv.at[s, p])

    half = length // 2

    def mine(s):
        return rows(2 * s + t, half)

    def theirs(s):
        return rows(2 * s + 1 - t, half)

    def dc_copy(n, i):
        here = theirs(n), cols(i, 256)
        return across(
            dc_snd.at[here], dc_rcv.at[here], x_send.at[0, n, i], x_recv.at[0, n, i]
        )

    def da_copy(s, i):
        here = theirs(s), cols(i, 256)
        return across(
            da_snd.at[here], da_rcv.at[here], x_send.at[1, s, i], x_recv.at[1, s, i]
        )

    def mlp_copy(s, i):
        here = rows(s, length), cols(i, 256)
        return across(
            mlp_snd.at[here], mlp_rcv.at[here], x_send.at[2, s, i], x_recv.at[2, s, i]
        )

    def do_copy(s):
        return across(do_snd.at[rows(s, half)], do_buf.at[mine(s)], y_send.at[s], y_recv.at[s])

    def gt_copy(s):
        here = gtok_ref.at[mine(s)]
        return across(here, here, y_send.at[2 + s], y_recv.at[2 + s])

    def fo_copy():
        return across(fo_buf.at[0], fo_buf.at[1], y_send.at[4], y_recv.at[4])

    wide = width // 256

    vacc[...] = jnp.zeros(vacc.shape, F32)
    vin[0:2] = gain_ref[...].astype(F32)
    vin[2:4] = shift_ref[...].astype(F32)
    vin[4:5] = ob_ref[...].astype(F32).reshape(1, width)
    vin[5:6] = mb_ref[...].astype(F32).reshape(1, width)
    line = hb_ref[...].astype(F32).reshape(1, hidden)
    vin[6:7] = line[:, :width]
    vin[7:8] = line[:, width:]
    vin[8:9, :local] = qvb_ref[0:1].astype(F32)
    vin[8:9, local:] = qvb_ref[1:2].astype(F32)

    lane = lax.broadcasted_iota(jnp.int32, (1, 128), 1)
    low_half = lane < HEAD

    def stacked(value):
        zero = jnp.zeros_like(value)
        return jnp.concatenate(
            [jnp.where(low_half, value, zero), jnp.where(low_half, zero, value)], axis=0
        )

    def normalize(value):
        mean = jnp.sum(value, axis=-1, keepdims=True) * (1.0 / width)
        center = value - mean
        spread = jnp.sum(center * center, axis=-1, keepdims=True) * (1.0 / width)
        scale_back = lax.rsqrt(spread + NORM_EPS)
        return center * scale_back, scale_back

    def norm_back(grad, normed, scale_back, gain):
        inner = grad * gain
        mean_one = jnp.sum(inner, axis=-1, keepdims=True) * (1.0 / width)
        mean_two = jnp.sum(inner * normed, axis=-1, keepdims=True) * (1.0 / width)
        return scale_back * (inner - mean_one - normed * mean_two)

    def same_image(s):
        ids = seg_ref[s : s + 1].astype(F32)
        down = jnp.broadcast_to(ids, (128, length)).T
        return jnp.concatenate(
            [down == ids[:, i * 128 : (i + 1) * 128] for i in range(length // 128)], axis=1
        )

    def norm_one(s):
        def step(i):
            here = rows(s * (length // CHUNK) + i, CHUNK)
            normed, scale_back = normalize(tok[here].astype(F32))
            xh1[here] = normed
            r1[here] = scale_back
            a_buf[here] = (normed * vin[0:1] + vin[2:3]).astype(BF)

        each(length // CHUNK, step)

    def attention(s, after):
        seq = rows(s, length)
        allowed = same_image(s)

        def pair_step(p):
            bias = jnp.concatenate(
                [
                    vin[8:9, cols(p, 128)],
                    jnp.zeros((1, 128), F32),
                    vin[8:9, cols(pairs + p, 128)],
                ],
                axis=1,
            )
            mixed = (dot(a_buf[seq], wq[:, cols(p, 384)], NN) + bias).astype(BF)
            qkv[seq, cols(p, 384)] = mixed
            scores = dot(mixed[:, :128], stacked(mixed[:, 128:256]), NT) * scale
            soft = []
            for e in range(2):
                one = jnp.where(allowed, scores[:, e * length : (e + 1) * length], MASKED)
                expo = jnp.exp(one - jnp.max(one, axis=-1, keepdims=True))
                soft.append(expo * (1.0 / jnp.sum(expo, axis=-1, keepdims=True)))
            both = jnp.concatenate(soft, axis=1)
            p_buf[s * pairs + p] = both
            o_buf[t, seq, cols(p, 128)] = dot(
                both.astype(BF), stacked(mixed[:, 256:]), NN
            ).astype(BF)
            o_copy(s, p).start()
            after(p)

        each(pairs, pair_step)

    tok_load.wait()
    norm_one(0)
    norm_one(1)
    pl.semaphore_wait(barrier, BITS + 1)
    wo_copy(0, 0).start()
    wo_copy(0, 1).start()
    for copy in wq_loads:
        copy.wait()
    attention(0, lambda p: None)

    def bring(p):
        if p > 0:
            wo_share(p - 1)

    attention(1, bring)

    strip = width // WAYS
    received = [r0_buf, r1_buf, r2_buf, r3_buf]

    def product(piece, left, right, order):
        full = dot(left, right, TN)
        for k in range(WAYS):
            b = [(k >> i) & 1 for i in order]
            grads[piece, b[0], b[1], b[2], b[3]] = full[k * strip : (k + 1) * strip].astype(BF)
        g_copy(piece, 0, order).start()

    def own(piece, depth, order):
        return (piece,) + tuple(bit[b] for b in order[:depth])

    def g_copy(piece, k, order):
        return toward(
            order[k],
            grads.at[own(piece, k, order) + (1 - bit[order[k]],)],
            received[k].at[piece],
            g_send.at[piece, k],
            g_recv.at[piece, k],
        )

    def pass_on(piece, k, order):
        g_copy(piece, k, order).wait_recv()
        here = own(piece, k + 1, order)
        grads[here] = (grads[here].astype(F32) + received[k][piece].astype(F32)).astype(BF)
        g_copy(piece, k + 1, order).start()

    def finish(piece, order):
        g_copy(piece, 3, order).wait_recv()
        return grads[own(piece, 4, order)].astype(F32) + received[3][piece].astype(F32)

    hidden_pieces = hidden // TILE
    down, into, outs, mixes = 0, hidden_pieces, 2 * hidden_pieces, 2 * hidden_pieces + 1
    others = mixes + pairs
    total = others + 1

    dy_load.wait()
    vacc[3:4] += jnp.sum(dy[...].astype(F32), axis=0, keepdims=True)
    wdn_load.wait()

    def hidden_back(i):
        back_buf[:, cols(i, 256)] = dot(dy[...], wdn[:, cols(i, 256)], NN)

    each(hidden // 256, hidden_back)
    wo_load.wait()
    win_load.wait()
    for part in range(2):
        wo_forward(part)
    for part in range(2):
        wo_copy(1, part).wait_recv()
        wo_copy(3, part).wait_recv()

    def middle(n):
        here = rows(n, BLOCK)

        for p in range(pairs):
            o_copy(n, p).wait_recv()

        h_buf[here] = dot(o_buf[0, here], wo[0], NT) + dot(o_buf[1, here], wo[1], NT)

        def norm_step(i):
            few = rows(n * (BLOCK // CHUNK) + i, CHUNK)
            resid = h_buf[few] + vin[4:5] + tok[few].astype(F32)
            h_buf[few] = resid
            normed, scale_back = normalize(resid)
            xh2[few] = normed
            r2[few] = scale_back
            c_buf[few] = (normed * vin[1:2] + vin[3:4]).astype(BF)

        each(BLOCK // CHUNK, norm_step)

        for m in range(hidden // width):

            def hidden_step(i, m=m):
                there = cols(i, 256)
                part = cols(m * wide + i, 256)
                pre = dot(c_buf[here], win[:, part], NN) + vin[6 + m : 7 + m, there]
                phi = 0.5 + 0.5 * lax.erf(pre * 0.7071067811865476)
                g_buf[here, part] = (pre * phi).astype(BF)
                slope = phi + pre * (jnp.exp(-0.5 * pre * pre) * 0.3989422804014327)
                low = (back_buf[here, part] * slope).astype(BF)
                du_buf[here, part] = low
                vacc[1 + m : 2 + m, there] += jnp.sum(low.astype(F32), axis=0, keepdims=True)

            each(wide, hidden_step)

    def normed_back(n):
        here = rows(n, BLOCK)

        def back_step(i):
            there = cols(i, 256)
            grad = dot(du_buf[here], win[rows(i, 256)], NT)
            dc_snd[here, there] = grad.astype(BF)
            dc_copy(n, i).start()
            vacc[10:11, there] += jnp.sum(grad * xh2[here, there], axis=0, keepdims=True)
            vacc[12:13, there] += jnp.sum(grad, axis=0, keepdims=True)

        each(wide, back_step)

    middle(0)
    normed_back(0)
    middle(1)

    def mlp_out(s):
        seq = rows(s, length)

        def step(i):
            mlp_snd[seq, cols(i, 256)] = dot(g_buf[seq], wdn[rows(i, 256)], NT).astype(BF)
            mlp_copy(s, i).start()

        each(wide, step)

    def resid_back(s):
        for i in range(wide):
            dc_copy(s, i).wait_recv()

        def step(i):
            here = rows((2 * s + t) * (half // CHUNK) + i, CHUNK)
            grad = dc_snd[here].astype(F32) + dc_rcv[here].astype(F32)
            full = dy[here].astype(F32) + norm_back(grad, xh2[here], r2[here], vin[1:2])
            xh2[here] = full
            dhb[rows(s * (half // CHUNK) + i, CHUNK)] = full.astype(BF)
            vacc[8:9] += jnp.sum(full, axis=0, keepdims=True)

        each(half // CHUNK, step)
        low = dhb[rows(s, half)]
        do_snd[rows(s, half)] = dot(low, wo[1 - t], NN).astype(BF)
        do_copy(s).start()
        do_buf[mine(s)] = dot(low, wo[t], NN).astype(BF)

    def attention_back(s, p):
        seq = rows(s, length)
        if (s, p) in heads_first:
            do_copy(s).wait_recv()
        mixed = qkv[seq, cols(p, 384)]
        query, keys = mixed[:, :128], stacked(mixed[:, 128:256])
        grad_o = do_buf[seq, cols(p, 128)]
        soft = p_buf[s * pairs + p]
        grad_soft = dot(grad_o, stacked(mixed[:, 256:]), NT)
        parts = []
        for e in range(2):
            one, two = (v[:, e * length : (e + 1) * length] for v in (soft, grad_soft))
            delta = jnp.sum(one * two, axis=-1, keepdims=True)
            parts.append((one * (two - delta)).astype(BF))
        grad_scores = jnp.concatenate(parts, axis=1)
        grad_query = dot(grad_scores, keys, NN) * scale
        grad_keys = dot(grad_scores, query, TN) * scale
        grad_keys = jnp.where(low_half, grad_keys[:length], grad_keys[length:])
        grad_values = dot(soft.astype(BF), grad_o, TN)
        grad_values = jnp.where(low_half, grad_values[:length], grad_values[length:])
        low = [v.astype(BF) for v in (grad_query, grad_keys, grad_values)]
        dp_buf[seq, cols(p, 384)] = jnp.concatenate(low, axis=1)
        vacc[0:1, cols(p, 128)] += jnp.sum(low[0].astype(F32), axis=0, keepdims=True)
        vacc[0:1, cols(pairs + p, 128)] += jnp.sum(low[2].astype(F32), axis=0, keepdims=True)

    def mixed_back(s):
        seq = rows(s, length)

        def step(i):
            here = cols(i, 256)
            grad = dot(dp_buf[seq], wq[rows(i, 256)], NT)
            da_snd[seq, here] = grad.astype(BF)
            vacc[9:10, here] += jnp.sum(grad * xh1[seq, here], axis=0, keepdims=True)
            vacc[11:12, here] += jnp.sum(grad, axis=0, keepdims=True)

        each(wide, step)

    def send_mixed(s):
        for i in range(wide):
            da_copy(s, i).start()

    def finish_block(s):
        seq = rows(s, length)

        def step(i):
            mlp_copy(s, i).wait_recv()
            here = seq, cols(i, 256)
            added = mlp_snd[here].astype(F32) + mlp_rcv[here].astype(F32)
            block_ref[seq, cols(i, 256)] = (h_buf[here] + (added + vin[5:6, cols(i, 256)])).astype(BF)

        each(wide, step)

    def finish_tokens(s):
        for i in range(wide):
            da_copy(s, i).wait_recv()

        def step(i):
            here = rows((2 * s + t) * (half // CHUNK) + i, CHUNK)
            grad = da_snd[here].astype(F32) + da_rcv[here].astype(F32)
            full = xh2[here] + norm_back(grad, xh1[here], r1[here], vin[0:1])
            gtok_ref[here] = full.astype(BF)

        each(half // CHUNK, step)
        gt_copy(s).start()

    def v_copy(k):
        sems = v_send.at[k], v_recv.at[k]
        if k == 0:
            shared = pl.ds(8, 8)
            return across(vsum.at[0, shared], vrcv.at[0, shared], *sems)
        return toward(k - 1, vsum.at[k], vrcv.at[k], *sems)

    def v_next(k):
        v_copy(k).wait_recv()
        if k == 0:
            vsum[1, :8] = vsum[0, :8]
            vsum[1, 8:] = vsum[0, 8:] + vrcv[0, 8:]
        else:
            vsum[k + 1] = vsum[k] + vrcv[k]
        if k < BITS:
            v_copy(k + 1).start()

    def prod(piece):
        order = HALVINGS[piece]
        if piece < into:
            product(piece, dy[...], g_buf[:, cols(piece, TILE)], order)
        elif piece < outs:
            product(piece, c_buf[...], du_buf[:, cols(piece - into, TILE)], order)
        elif piece in (outs, others):
            side = t if piece == outs else 1 - t
            heads = jnp.concatenate([o_buf[side, mine(s)] for s in range(seqs)], axis=0)
            product(piece, dhb[...], heads, order)
        else:
            product(piece, a_buf[...], dp_buf[:, cols(piece - mixes, 384)], order)

    def fin(piece):
        value = finish(piece, HALVINGS[piece])
        if piece < into:
            gdn_ref[:, cols(piece, TILE)] = value
        elif piece < outs:
            gin_ref[:, cols(piece - into, TILE)] = value
        else:
            for kind in range(3):
                gqkv_ref[kind, :, cols(piece - mixes, 128)] = value[:, cols(kind, 128)]

    def outer_send():
        fo_buf[0] = finish(others, HALVINGS[others]).astype(BF)
        fo_copy().start()

    def outer_end():
        value = finish(outs, HALVINGS[outs])
        fo_copy().wait_recv()
        gout_ref[...] = value + fo_buf[1].astype(F32)

    heads_first = {}
    for name, *which in PLAN:
        if name == "attb":
            heads_first.setdefault(which[0], tuple(which))
    heads_first = tuple(heads_first.values())

    def small(k):
        if k == 0:
            v_copy(0).start()
        else:
            v_next(k - 1)
        if k == BITS + 1:
            vout[...] = vsum[k]

    steps = {
        "prod": prod,
        "pass": lambda piece, k: pass_on(piece, k, HALVINGS[piece]),
        "fin": fin,
        "mb": normed_back,
        "resid": resid_back,
        "attb": attention_back,
        "mixb": mixed_back,
        "sda": send_mixed,
        "mlp": mlp_out,
        "fb": finish_block,
        "ft": finish_tokens,
        "gt": lambda s: gt_copy(s).wait_recv(),
        "fo": outer_send,
        "foe": outer_end,
        "v": small,
    }
    for name, *which in PLAN:
        steps[name](*which)

    for part in range(2):
        for step in range(4):
            wo_copy(step, part).wait_send()
    for s in range(seqs):
        for p in range(pairs):
            o_copy(s, p).wait_send()
        for i in range(wide):
            da_copy(s, i).wait_send()
            mlp_copy(s, i).wait_send()
            dc_copy(s, i).wait_send()
        do_copy(s).wait_send()
        gt_copy(s).wait_send()
    fo_copy().wait_send()
    for piece in range(total):
        for k in range(BITS):
            g_copy(piece, k, HALVINGS[piece]).wait_send()
    for k in range(BITS + 1):
        v_copy(k).wait_send()


def deliver(
    block_v,
    gtok_v,
    gqkv_v,
    gout_v,
    gin_v,
    gdn_v,
    small,
    block_o,
    gtok_o,
    gqkv_o,
    pair_o,
    gout_o,
    ob_o,
    gin_o,
    hb_o,
    gdn_o,
    mb_o,
    gain_o,
    shift_o,
    sem,
):
    big = (
        (block_v, block_o),
        (gtok_v, gtok_o),
        (gqkv_v, gqkv_o),
        (gout_v, gout_o),
        (gin_v, gin_o),
        (gdn_v, gdn_o),
    )
    copies = [pltpu.make_async_copy(src, dst, sem.at[i]) for i, (src, dst) in enumerate(big)]
    for copy in copies:
        copy.start()
    local, width, hidden = pair_o.shape[1], ob_o.shape[0], hb_o.shape[0]
    pair_o[0:1] = small[0:1, :local]
    pair_o[1:2] = small[0:1, local:]
    hb_o[...] = jnp.concatenate([small[1:2], small[2:3]], axis=1).reshape(hidden)
    ob_o[...] = small[8:9].reshape(width)
    mb_o[...] = small[3:4].reshape(width)
    gain_o[...] = small[9:11]
    shift_o[...] = small[11:13]
    for copy in copies:
        copy.wait()


def body(
    tokens,
    segment_ids,
    w_qkv,
    qv_bias,
    w_out,
    out_bias,
    w_in,
    hidden_bias,
    w_down,
    mlp_bias,
    ln_gain,
    ln_bias,
    cotangent,
    *,
    dp,
):
    seqs, length, width = tokens.shape
    count = seqs * length
    local = w_qkv.shape[2]
    hidden = w_in.shape[1]
    pairs = local // (2 * HEAD)
    stride = dp // WAYS
    strip = width // WAYS
    pieces = 2 * (hidden // TILE) + 2 + pairs
    hbm = pl.BlockSpec(memory_space=pl.ANY)
    vmem = pl.BlockSpec(memory_space=pltpu.VMEM)
    dma = pltpu.SemaphoreType.DMA
    wide = (count, width)
    big = (
        pltpu.VMEM(wide, BF),
        pltpu.VMEM(wide, BF),
        pltpu.VMEM((3, strip, local), F32),
        pltpu.VMEM((strip, local), F32),
        pltpu.VMEM((strip, hidden), F32),
        pltpu.VMEM((strip, hidden), F32),
    )
    outs = pl.pallas_call(
        functools.partial(kernel, stride),
        out_shape=big + (pltpu.VMEM((16, width), F32),),
        in_specs=[hbm, vmem, hbm, vmem, hbm, vmem, hbm, vmem, hbm, vmem, vmem, vmem, hbm],
        out_specs=(vmem,) * 7,
        scratch_shapes=[
            pltpu.VMEM(wide, BF),
            pltpu.VMEM(wide, BF),
            pltpu.VMEM((width, 3 * local), BF),
            pltpu.VMEM((2, width, local), BF),
            pltpu.VMEM((width, hidden), BF),
            pltpu.VMEM((width, hidden), BF),
            pltpu.VMEM((16, width), F32),
            pltpu.VMEM(wide, BF),
            pltpu.VMEM(wide, F32),
            pltpu.VMEM((count, 1), F32),
            pltpu.VMEM((count, 3 * local), BF),
            pltpu.VMEM((seqs * pairs, length, 2 * length), F32),
            pltpu.VMEM((2, count, local), BF),
            pltpu.VMEM(wide, F32),
            pltpu.VMEM(wide, F32),
            pltpu.VMEM((count, 1), F32),
            pltpu.VMEM(wide, BF),
            pltpu.VMEM((count, hidden), F32),
            pltpu.VMEM((count, hidden), BF),
            pltpu.VMEM((count, hidden), BF),
            pltpu.VMEM(wide, BF),
            pltpu.VMEM(wide, BF),
            pltpu.VMEM(wide, BF),
            pltpu.VMEM(wide, BF),
            pltpu.VMEM(wide, BF),
            pltpu.VMEM(wide, BF),
            pltpu.VMEM((count, local), BF),
            pltpu.VMEM((count // 2, local), BF),
            pltpu.VMEM((count // 2, width), BF),
            pltpu.VMEM((2, strip, local), BF),
            pltpu.VMEM((count, 3 * local), BF),
            pltpu.VMEM((pieces, 2, 2, 2, 2, strip, TILE), BF),
            pltpu.VMEM((pieces, 2, 2, 2, strip, TILE), BF),
            pltpu.VMEM((pieces, 2, 2, strip, TILE), BF),
            pltpu.VMEM((pieces, 2, strip, TILE), BF),
            pltpu.VMEM((pieces, strip, TILE), BF),
            pltpu.VMEM((BITS + 2, 16, width), F32),
            pltpu.VMEM((BITS + 1, 16, width), F32),
            dma((5 + 3 * pairs,)),
            dma((4, 2)),
            dma((4, 2)),
            dma((seqs, pairs)),
            dma((seqs, pairs)),
            dma((3, count // BLOCK, width // 256)),
            dma((3, count // BLOCK, width // 256)),
            dma((5,)),
            dma((5,)),
            dma((pieces, BITS)),
            dma((pieces, BITS)),
            dma((BITS + 1,)),
            dma((BITS + 1,)),
        ],
        compiler_params=pltpu.CompilerParams(
            collective_id=0, has_side_effects=True, vmem_limit_bytes=58 * 2**20
        ),
        cost_estimate=pl.CostEstimate(
            flops=12 * 10**9, bytes_accessed=12 * 10**6, transcendentals=4 * 10**6
        ),
    )(
        tokens.reshape(wide),
        segment_ids,
        w_qkv.transpose(1, 0, 2),
        qv_bias,
        w_out,
        out_bias,
        w_in,
        hidden_bias,
        w_down,
        mlp_bias,
        ln_gain,
        ln_bias,
        cotangent.reshape(wide),
    )
    if stride > 1:
        groups = [[g * stride + i for i in range(stride)] for g in range(WAYS)]
        scatter = functools.partial(
            lax.psum_scatter, axis_name="dp", axis_index_groups=groups, tiled=True
        )
        outs = (
            *outs[:2],
            scatter(outs[2], scatter_dimension=1),
            *[scatter(v, scatter_dimension=0) for v in outs[3:6]],
            lax.psum(outs[6], "dp", axis_index_groups=groups),
        )
    shapes = [
        outs[0],
        outs[1],
        outs[2],
        jax.ShapeDtypeStruct((2, local), F32),
        outs[3],
        jax.ShapeDtypeStruct((width,), F32),
        outs[4],
        jax.ShapeDtypeStruct((hidden,), F32),
        outs[5],
        jax.ShapeDtypeStruct((width,), F32),
        jax.ShapeDtypeStruct((2, width), F32),
        jax.ShapeDtypeStruct((2, width), F32),
    ]
    placed = [hbm, hbm, hbm, vmem, hbm, vmem, hbm, vmem, hbm, vmem, vmem, vmem]
    done = pl.pallas_call(
        deliver,
        out_shape=tuple(jax.ShapeDtypeStruct(v.shape, v.dtype) for v in shapes),
        in_specs=[vmem] * 7,
        out_specs=tuple(placed),
        scratch_shapes=[dma((6,))],
    )(*[pltpu.with_memory_space_constraint(v, pltpu.VMEM) for v in outs])
    return (
        done[0].reshape(tokens.shape),
        done[1].reshape(tokens.shape),
        done[2].transpose(1, 0, 2),
        *done[3:],
    )


def solution(mesh):
    return jax.shard_map(
        functools.partial(body, dp=mesh.shape["dp"]),
        mesh=mesh,
        in_specs=(
            P("dp", None, None),
            P("dp", None),
            P(None, None, "tensor"),
            P(None, "tensor"),
            P(None, "tensor"),
            P(),
            P(None, "tensor"),
            P("tensor"),
            P(None, "tensor"),
            P(),
            P(),
            P(),
            P("dp", None, None),
        ),
        out_specs=(
            P("dp", None, None),
            P("dp", None, None),
            P("dp", None, "tensor"),
            P(None, "tensor"),
            P("dp", "tensor"),
            P(),
            P("dp", "tensor"),
            P("tensor"),
            P("dp", "tensor"),
            P(),
            P(),
            P(),
        ),
        check_vma=False,
    )
```

```python
import functools

import jax
import jax.numpy as jnp
from jax import lax
from jax.experimental import pallas as pl
from jax.experimental.pallas import tpu as pltpu
from jax.sharding import PartitionSpec as P

MESH = pl.DeviceIdType.MESH
BF = jnp.bfloat16
F32 = jnp.float32
HEAD = 64
NORM_EPS = 1e-06
MASKED = -1000000000.0
BITS = 4
WAYS = 2**BITS
BLOCK = 256
CHUNK = 64
TILE = 384

PLAN = (
    ("prod", 0), ("prod", 7), ("mb", 1), ("pass", 0, 0), ("prod", 4), ("pass", 7, 0), ("prod", 2),
    ("prod", 1), ("prod", 3), ("resid", 0), ("pass", 2, 0), ("pass", 3, 0), ("pass", 4, 0),
    ("pass", 1, 0), ("resid", 1), ("prod", 8), ("pass", 0, 1), ("prod", 12), ("pass", 8, 0),
    ("attb", 0, 1), ("mlp", 1), ("pass", 7, 1), ("attb", 1, 0), ("prod", 5), ("pass", 2, 1),
    ("pass", 3, 1), ("attb", 0, 0), ("attb", 0, 2), ("pass", 5, 0), ("attb", 1, 2), ("prod", 11),
    ("mixb", 0), ("pass", 1, 1), ("pass", 12, 0), ("pass", 0, 2), ("attb", 1, 1), ("mixb", 1),
    ("prod", 6), ("v", 0), ("pass", 2, 2), ("sda", 0), ("pass", 8, 1), ("pass", 3, 2),
    ("pass", 11, 0), ("prod", 9), ("prod", 10), ("pass", 5, 1), ("mlp", 0), ("pass", 6, 0),
    ("fb", 1), ("v", 1), ("v", 2), ("pass", 1, 2), ("pass", 12, 1), ("pass", 11, 1), ("sda", 1),
    ("pass", 8, 2), ("pass", 5, 2), ("pass", 9, 0), ("pass", 7, 2), ("v", 3), ("pass", 12, 2),
    ("pass", 10, 0), ("pass", 6, 1), ("pass", 11, 2), ("v", 4), ("ft", 0), ("fin", 3),
    ("pass", 4, 1), ("pass", 9, 1), ("pass", 6, 2), ("fo",), ("pass", 10, 1), ("fin", 0), ("ft", 1),
    ("pass", 4, 2), ("pass", 9, 2), ("fin", 5), ("fin", 1), ("pass", 10, 2), ("fb", 0), ("fin", 7),
    ("fin", 4), ("fin", 2), ("fin", 9), ("fin", 6), ("v", 5), ("foe",), ("fin", 11), ("fin", 10),
    ("gt", 0), ("gt", 1),
)
HALVINGS = (
    (0, 1, 2, 3),
    (0, 1, 2, 3),
    (0, 1, 2, 3),
    (0, 1, 2, 3),
    (0, 2, 1, 3),
    (0, 1, 2, 3),
    (0, 1, 2, 3),
    (0, 2, 1, 3),
    (0, 2, 1, 3),
    (0, 1, 2, 3),
    (0, 1, 2, 3),
    (0, 2, 1, 3),
    (0, 1, 2, 3),
)

NN = ((1,), (0,))
NT = ((1,), (1,))
TN = ((0,), (0,))


def dot(a, b, dims):
    return lax.dot_general(a, b, (dims, ((), ())), preferred_element_type=F32)


def each(count, step):
    for i in range(count):
        step(i)


def rows(i, size):
    if isinstance(i, int):
        return slice(i * size, (i + 1) * size)
    return pl.ds(pl.multiple_of(i * size, size), size)


cols = rows


def kernel(
    stride,
    tok_h,
    seg_ref,
    wqkv_h,
    qvb_ref,
    wout_h,
    ob_ref,
    win_h,
    hb_ref,
    wdn_h,
    mb_ref,
    gain_ref,
    shift_ref,
    dy_h,
    block_ref,
    gtok_ref,
    gqkv_ref,
    gout_ref,
    gin_ref,
    gdn_ref,
    vout,
    tok,
    dy,
    wq,
    wo,
    win,
    wdn,
    vin,
    a_buf,
    xh1,
    r1,
    qkv,
    p_buf,
    o_buf,
    h_buf,
    xh2,
    r2,
    c_buf,
    back_buf,
    g_buf,
    du_buf,
    dc_snd,
    dc_rcv,
    mlp_snd,
    mlp_rcv,
    da_snd,
    da_rcv,
    do_buf,
    do_snd,
    dhb,
    fo_buf,
    dp_buf,
    grads,
    r0_buf,
    r1_buf,
    r2_buf,
    r3_buf,
    vsum,
    vrcv,
    in_sem,
    wo_send,
    wo_recv,
    o_send,
    o_recv,
    x_send,
    x_recv,
    y_send,
    y_recv,
    g_send,
    g_recv,
    v_send,
    v_recv,
):
    d = lax.axis_index("dp")
    t = lax.axis_index("tensor")
    group = d // stride
    bit = [lax.rem(group // (2**b), 2) for b in range(BITS)]
    mate = [d + (1 - 2 * bit[b]) * (2**b) * stride for b in range(BITS)]
    count, width = tok.shape
    seqs = seg_ref.shape[0]
    length = count // seqs
    local = wo.shape[2]
    pairs = local // (2 * HEAD)
    hidden = win.shape[1]
    scale = HEAD ** (-0.5)
    vacc = vsum.at[0]

    barrier = pltpu.get_barrier_semaphore()
    pl.semaphore_signal(barrier, inc=1, device_id=(d, 1 - t), device_id_type=MESH)
    for b in range(BITS):
        pl.semaphore_signal(barrier, inc=1, device_id=(mate[b], t), device_id_type=MESH)

    loads = []

    def load(src, dst):
        copy = pltpu.make_async_copy(src, dst, in_sem.at[len(loads)])
        copy.start()
        loads.append(copy)
        return copy

    tok_load = load(tok_h, tok)
    wq_loads = [
        load(
            wqkv_h.at[kind, :, p * 128 : (p + 1) * 128],
            wq.at[:, p * 384 + kind * 128 : p * 384 + (kind + 1) * 128],
        )
        for p in range(pairs)
        for kind in range(3)
    ]
    dy_load = load(dy_h, dy)
    wo_load = load(wout_h, wo.at[t])
    win_load = load(win_h, win)
    wdn_load = load(wdn_h, wdn)

    def across(src, dst, send, recv):
        return pltpu.make_async_remote_copy(
            src_ref=src,
            dst_ref=dst,
            send_sem=send,
            recv_sem=recv,
            device_id=(d, 1 - t),
            device_id_type=MESH,
        )

    def toward(b, src, dst, send, recv):
        return pltpu.make_async_remote_copy(
            src_ref=src,
            dst_ref=dst,
            send_sem=send,
            recv_sem=recv,
            device_id=(mate[b], t),
            device_id_type=MESH,
        )

    slab = width // 8

    def wo_rows(turned, part):
        first = bit[0]
        second = 1 - bit[1] if turned else bit[1]
        return rows((2 * second + first) * 2 + part, slab)

    def wo_copy(step, part):
        sems = wo_send.at[step, part], wo_recv.at[step, part]
        if step == 0:
            here = wo_rows(False, part)
            return across(wout_h.at[here], wo.at[t, here], *sems)
        here = wo_rows(step == 3, part)
        return toward(1 if step == 2 else 0, wo.at[1 - t, here], wo.at[1 - t, here], *sems)

    def wo_share(part):
        wo_copy(0, part).wait_recv()
        wo_copy(2, part).start()
        wo_copy(1, part).start()

    def wo_forward(part):
        wo_copy(2, part).wait_recv()
        wo_copy(3, part).start()

    def o_copy(s, p):
        here = rows(s, length)
        place = o_buf.at[t, here, cols(p, 128)]
        return across(place, place, o_send.at[s, p], o_recv.at[s, p])

    half = length // 2

    def mine(s):
        return rows(2 * s + t, half)

    def theirs(s):
        return rows(2 * s + 1 - t, half)

    def dc_copy(n, i):
        here = theirs(n), cols(i, 256)
        return across(
            dc_snd.at[here], dc_rcv.at[here], x_send.at[0, n, i], x_recv.at[0, n, i]
        )

    def da_copy(s, i):
        here = theirs(s), cols(i, 256)
        return across(
            da_snd.at[here], da_rcv.at[here], x_send.at[1, s, i], x_recv.at[1, s, i]
        )

    def mlp_copy(s, i):
        here = rows(s, length), cols(i, 256)
        return across(
            mlp_snd.at[here], mlp_rcv.at[here], x_send.at[2, s, i], x_recv.at[2, s, i]
        )

    def do_copy(s):
        return across(do_snd.at[rows(s, half)], do_buf.at[mine(s)], y_send.at[s], y_recv.at[s])

    def gt_copy(s):
        here = gtok_ref.at[mine(s)]
        return across(here, here, y_send.at[2 + s], y_recv.at[2 + s])

    def fo_copy():
        return across(fo_buf.at[0], fo_buf.at[1], y_send.at[4], y_recv.at[4])

    wide = width // 256

    vacc[...] = jnp.zeros(vacc.shape, F32)
    vin[0:2] = gain_ref[...].astype(F32)
    vin[2:4] = shift_ref[...].astype(F32)
    vin[4:5] = ob_ref[...].astype(F32).reshape(1, width)
    vin[5:6] = mb_ref[...].astype(F32).reshape(1, width)
    line = hb_ref[...].astype(F32).reshape(1, hidden)
    vin[6:7] = line[:, :width]
    vin[7:8] = line[:, width:]
    vin[8:9, :local] = qvb_ref[0:1].astype(F32)
    vin[8:9, local:] = qvb_ref[1:2].astype(F32)

    lane = lax.broadcasted_iota(jnp.int32, (1, 128), 1)
    low_half = lane < HEAD

    def stacked(value):
        zero = jnp.zeros_like(value)
        return jnp.concatenate(
            [jnp.where(low_half, value, zero), jnp.where(low_half, zero, value)], axis=0
        )

    def normalize(value):
        mean = jnp.sum(value, axis=-1, keepdims=True) * (1.0 / width)
        center = value - mean
        spread = jnp.sum(center * center, axis=-1, keepdims=True) * (1.0 / width)
        scale_back = lax.rsqrt(spread + NORM_EPS)
        return center * scale_back, scale_back

    def norm_back(grad, normed, scale_back, gain):
        inner = grad * gain
        mean_one = jnp.sum(inner, axis=-1, keepdims=True) * (1.0 / width)
        mean_two = jnp.sum(inner * normed, axis=-1, keepdims=True) * (1.0 / width)
        return scale_back * (inner - mean_one - normed * mean_two)

    def same_image(s):
        ids = seg_ref[s : s + 1].astype(F32)
        down = jnp.broadcast_to(ids, (128, length)).T
        return jnp.concatenate(
            [down == ids[:, i * 128 : (i + 1) * 128] for i in range(length // 128)], axis=1
        )

    def norm_one(s):
        def step(i):
            here = rows(s * (length // CHUNK) + i, CHUNK)
            normed, scale_back = normalize(tok[here].astype(F32))
            xh1[here] = normed
            r1[here] = scale_back
            a_buf[here] = (normed * vin[0:1] + vin[2:3]).astype(BF)

        each(length // CHUNK, step)

    def attention(s, after):
        seq = rows(s, length)
        allowed = same_image(s)

        def pair_step(p):
            bias = jnp.concatenate(
                [
                    vin[8:9, cols(p, 128)],
                    jnp.zeros((1, 128), F32),
                    vin[8:9, cols(pairs + p, 128)],
                ],
                axis=1,
            )
            mixed = (dot(a_buf[seq], wq[:, cols(p, 384)], NN) + bias).astype(BF)
            qkv[seq, cols(p, 384)] = mixed
            scores = dot(mixed[:, :128], stacked(mixed[:, 128:256]), NT) * scale
            soft = []
            for e in range(2):
                one = jnp.where(allowed, scores[:, e * length : (e + 1) * length], MASKED)
                expo = jnp.exp(one - jnp.max(one, axis=-1, keepdims=True))
                soft.append(expo * (1.0 / jnp.sum(expo, axis=-1, keepdims=True)))
            both = jnp.concatenate(soft, axis=1)
            p_buf[s * pairs + p] = both
            o_buf[t, seq, cols(p, 128)] = dot(
                both.astype(BF), stacked(mixed[:, 256:]), NN
            ).astype(BF)
            o_copy(s, p).start()
            after(p)

        each(pairs, pair_step)

    tok_load.wait()
    norm_one(0)
    norm_one(1)
    pl.semaphore_wait(barrier, BITS + 1)
    wo_copy(0, 0).start()
    wo_copy(0, 1).start()
    for copy in wq_loads:
        copy.wait()
    attention(0, lambda p: None)

    def bring(p):
        if p > 0:
            wo_share(p - 1)

    attention(1, bring)

    strip = width // WAYS
    received = [r0_buf, r1_buf, r2_buf, r3_buf]

    def product(piece, left, right, order):
        full = dot(left, right, TN)
        for k in range(WAYS):
            b = [(k >> i) & 1 for i in order]
            grads[piece, b[0], b[1], b[2], b[3]] = full[k * strip : (k + 1) * strip].astype(BF)
        g_copy(piece, 0, order).start()

    def own(piece, depth, order):
        return (piece,) + tuple(bit[b] for b in order[:depth])

    def g_copy(piece, k, order):
        return toward(
            order[k],
            grads.at[own(piece, k, order) + (1 - bit[order[k]],)],
            received[k].at[piece],
            g_send.at[piece, k],
            g_recv.at[piece, k],
        )

    def pass_on(piece, k, order):
        g_copy(piece, k, order).wait_recv()
        here = own(piece, k + 1, order)
        grads[here] = (grads[here].astype(F32) + received[k][piece].astype(F32)).astype(BF)
        g_copy(piece, k + 1, order).start()

    def finish(piece, order):
        g_copy(piece, 3, order).wait_recv()
        return grads[own(piece, 4, order)].astype(F32) + received[3][piece].astype(F32)

    hidden_pieces = hidden // TILE
    down, into, outs, mixes = 0, hidden_pieces, 2 * hidden_pieces, 2 * hidden_pieces + 1
    others = mixes + pairs
    total = others + 1

    dy_load.wait()
    vacc[3:4] += jnp.sum(dy[...].astype(F32), axis=0, keepdims=True)
    wdn_load.wait()

    def hidden_back(i):
        back_buf[:, cols(i, 256)] = dot(dy[...], wdn[:, cols(i, 256)], NN)

    each(hidden // 256, hidden_back)
    wo_load.wait()
    win_load.wait()
    for part in range(2):
        wo_forward(part)
    for part in range(2):
        wo_copy(1, part).wait_recv()
        wo_copy(3, part).wait_recv()

    def middle(n):
        here = rows(n, BLOCK)

        for p in range(pairs):
            o_copy(n, p).wait_recv()

        h_buf[here] = dot(o_buf[0, here], wo[0], NT) + dot(o_buf[1, here], wo[1], NT)

        def norm_step(i):
            few = rows(n * (BLOCK // CHUNK) + i, CHUNK)
            resid = h_buf[few] + vin[4:5] + tok[few].astype(F32)
            h_buf[few] = resid
            normed, scale_back = normalize(resid)
            xh2[few] = normed
            r2[few] = scale_back
            c_buf[few] = (normed * vin[1:2] + vin[3:4]).astype(BF)

        each(BLOCK // CHUNK, norm_step)

        for m in range(hidden // width):

            def hidden_step(i, m=m):
                there = cols(i, 256)
                part = cols(m * wide + i, 256)
                pre = dot(c_buf[here], win[:, part], NN) + vin[6 + m : 7 + m, there]
                phi = 0.5 + 0.5 * lax.erf(pre * 0.7071067811865476)
                g_buf[here, part] = (pre * phi).astype(BF)
                slope = phi + pre * (jnp.exp(-0.5 * pre * pre) * 0.3989422804014327)
                low = (back_buf[here, part] * slope).astype(BF)
                du_buf[here, part] = low
                vacc[1 + m : 2 + m, there] += jnp.sum(low.astype(F32), axis=0, keepdims=True)

            each(wide, hidden_step)

    def normed_back(n):
        here = rows(n, BLOCK)

        def back_step(i):
            there = cols(i, 256)
            grad = dot(du_buf[here], win[rows(i, 256)], NT)
            dc_snd[here, there] = grad.astype(BF)
            dc_copy(n, i).start()
            vacc[10:11, there] += jnp.sum(grad * xh2[here, there], axis=0, keepdims=True)
            vacc[12:13, there] += jnp.sum(grad, axis=0, keepdims=True)

        each(wide, back_step)

    middle(0)
    normed_back(0)
    middle(1)

    def mlp_out(s):
        seq = rows(s, length)

        def step(i):
            mlp_snd[seq, cols(i, 256)] = dot(g_buf[seq], wdn[rows(i, 256)], NT).astype(BF)
            mlp_copy(s, i).start()

        each(wide, step)

    def resid_back(s):
        for i in range(wide):
            dc_copy(s, i).wait_recv()

        def step(i):
            here = rows((2 * s + t) * (half // CHUNK) + i, CHUNK)
            grad = dc_snd[here].astype(F32) + dc_rcv[here].astype(F32)
            full = dy[here].astype(F32) + norm_back(grad, xh2[here], r2[here], vin[1:2])
            xh2[here] = full
            dhb[rows(s * (half // CHUNK) + i, CHUNK)] = full.astype(BF)
            vacc[8:9] += jnp.sum(full, axis=0, keepdims=True)

        each(half // CHUNK, step)
        low = dhb[rows(s, half)]
        do_snd[rows(s, half)] = dot(low, wo[1 - t], NN).astype(BF)
        do_copy(s).start()
        do_buf[mine(s)] = dot(low, wo[t], NN).astype(BF)

    def attention_back(s, p):
        seq = rows(s, length)
        if (s, p) in heads_first:
            do_copy(s).wait_recv()
        mixed = qkv[seq, cols(p, 384)]
        query, keys = mixed[:, :128], stacked(mixed[:, 128:256])
        grad_o = do_buf[seq, cols(p, 128)]
        soft = p_buf[s * pairs + p]
        grad_soft = dot(grad_o, stacked(mixed[:, 256:]), NT)
        parts = []
        for e in range(2):
            one, two = (v[:, e * length : (e + 1) * length] for v in (soft, grad_soft))
            delta = jnp.sum(one * two, axis=-1, keepdims=True)
            parts.append((one * (two - delta)).astype(BF))
        grad_scores = jnp.concatenate(parts, axis=1)
        grad_query = dot(grad_scores, keys, NN) * scale
        grad_keys = dot(grad_scores, query, TN) * scale
        grad_keys = jnp.where(low_half, grad_keys[:length], grad_keys[length:])
        grad_values = dot(soft.astype(BF), grad_o, TN)
        grad_values = jnp.where(low_half, grad_values[:length], grad_values[length:])
        low = [v.astype(BF) for v in (grad_query, grad_keys, grad_values)]
        dp_buf[seq, cols(p, 384)] = jnp.concatenate(low, axis=1)
        vacc[0:1, cols(p, 128)] += jnp.sum(low[0].astype(F32), axis=0, keepdims=True)
        vacc[0:1, cols(pairs + p, 128)] += jnp.sum(low[2].astype(F32), axis=0, keepdims=True)

    def mixed_back(s):
        seq = rows(s, length)

        def step(i):
            here = cols(i, 256)
            grad = dot(dp_buf[seq], wq[rows(i, 256)], NT)
            da_snd[seq, here] = grad.astype(BF)
            vacc[9:10, here] += jnp.sum(grad * xh1[seq, here], axis=0, keepdims=True)
            vacc[11:12, here] += jnp.sum(grad, axis=0, keepdims=True)

        each(wide, step)

    def send_mixed(s):
        for i in range(wide):
            da_copy(s, i).start()

    def finish_block(s):
        seq = rows(s, length)

        def step(i):
            mlp_copy(s, i).wait_recv()
            here = seq, cols(i, 256)
            added = mlp_snd[here].astype(F32) + mlp_rcv[here].astype(F32)
            block_ref[seq, cols(i, 256)] = (h_buf[here] + (added + vin[5:6, cols(i, 256)])).astype(BF)

        each(wide, step)

    def finish_tokens(s):
        for i in range(wide):
            da_copy(s, i).wait_recv()

        def step(i):
            here = rows((2 * s + t) * (half // CHUNK) + i, CHUNK)
            grad = da_snd[here].astype(F32) + da_rcv[here].astype(F32)
            full = xh2[here] + norm_back(grad, xh1[here], r1[here], vin[0:1])
            gtok_ref[here] = full.astype(BF)

        each(half // CHUNK, step)
        gt_copy(s).start()

    def v_copy(k):
        sems = v_send.at[k], v_recv.at[k]
        if k == 0:
            shared = pl.ds(8, 8)
            return across(vsum.at[0, shared], vrcv.at[0, shared], *sems)
        return toward(k - 1, vsum.at[k], vrcv.at[k], *sems)

    def v_next(k):
        v_copy(k).wait_recv()
        if k == 0:
            vsum[1, :8] = vsum[0, :8]
            vsum[1, 8:] = vsum[0, 8:] + vrcv[0, 8:]
        else:
            vsum[k + 1] = vsum[k] + vrcv[k]
        if k < BITS:
            v_copy(k + 1).start()

    def prod(piece):
        order = HALVINGS[piece]
        if piece < into:
            product(piece, dy[...], g_buf[:, cols(piece, TILE)], order)
        elif piece < outs:
            product(piece, c_buf[...], du_buf[:, cols(piece - into, TILE)], order)
        elif piece in (outs, others):
            side = t if piece == outs else 1 - t
            heads = jnp.concatenate([o_buf[side, mine(s)] for s in range(seqs)], axis=0)
            product(piece, dhb[...], heads, order)
        else:
            product(piece, a_buf[...], dp_buf[:, cols(piece - mixes, 384)], order)

    def fin(piece):
        value = finish(piece, HALVINGS[piece])
        if piece < into:
            gdn_ref[:, cols(piece, TILE)] = value
        elif piece < outs:
            gin_ref[:, cols(piece - into, TILE)] = value
        else:
            for kind in range(3):
                gqkv_ref[kind, :, cols(piece - mixes, 128)] = value[:, cols(kind, 128)]

    def outer_send():
        fo_buf[0] = finish(others, HALVINGS[others]).astype(BF)
        fo_copy().start()

    def outer_end():
        value = finish(outs, HALVINGS[outs])
        fo_copy().wait_recv()
        gout_ref[...] = value + fo_buf[1].astype(F32)

    heads_first = {}
    for name, *which in PLAN:
        if name == "attb":
            heads_first.setdefault(which[0], tuple(which))
    heads_first = tuple(heads_first.values())

    def small(k):
        if k == 0:
            v_copy(0).start()
        else:
            v_next(k - 1)
        if k == BITS + 1:
            vout[...] = vsum[k]

    steps = {
        "prod": prod,
        "pass": lambda piece, k: pass_on(piece, k, HALVINGS[piece]),
        "fin": fin,
        "mb": normed_back,
        "resid": resid_back,
        "attb": attention_back,
        "mixb": mixed_back,
        "sda": send_mixed,
        "mlp": mlp_out,
        "fb": finish_block,
        "ft": finish_tokens,
        "gt": lambda s: gt_copy(s).wait_recv(),
        "fo": outer_send,
        "foe": outer_end,
        "v": small,
    }
    for name, *which in PLAN:
        steps[name](*which)

    for part in range(2):
        for step in range(4):
            wo_copy(step, part).wait_send()
    for s in range(seqs):
        for p in range(pairs):
            o_copy(s, p).wait_send()
        for i in range(wide):
            da_copy(s, i).wait_send()
            mlp_copy(s, i).wait_send()
            dc_copy(s, i).wait_send()
        do_copy(s).wait_send()
        gt_copy(s).wait_send()
    fo_copy().wait_send()
    for piece in range(total):
        for k in range(BITS):
            g_copy(piece, k, HALVINGS[piece]).wait_send()
    for k in range(BITS + 1):
        v_copy(k).wait_send()


def deliver(
    block_v,
    gtok_v,
    gqkv_v,
    gout_v,
    gin_v,
    gdn_v,
    small,
    block_o,
    gtok_o,
    gqkv_o,
    pair_o,
    gout_o,
    ob_o,
    gin_o,
    hb_o,
    gdn_o,
    mb_o,
    gain_o,
    shift_o,
    pair_m,
    ob_m,
    hb_m,
    mb_m,
    gain_m,
    shift_m,
    sem,
):
    big = (
        (block_v, block_o),
        (gtok_v, gtok_o),
        (gqkv_v, gqkv_o),
        (gout_v, gout_o),
        (gin_v, gin_o),
        (gdn_v, gdn_o),
    )
    copies = [pltpu.make_async_copy(src, dst, sem.at[i]) for i, (src, dst) in enumerate(big)]
    for copy in copies:
        copy.start()
    local, width, hidden = pair_o.shape[1], ob_o.shape[0], hb_o.shape[0]
    pair_m[0:1] = small[0:1, :local]
    pair_m[1:2] = small[0:1, local:]
    hb_m[...] = jnp.concatenate([small[1:2], small[2:3]], axis=1).reshape(hidden)
    ob_m[...] = small[8:9].reshape(width)
    mb_m[...] = small[3:4].reshape(width)
    gain_m[...] = small[9:11]
    shift_m[...] = small[11:13]
    little = (
        (pair_m, pair_o),
        (ob_m, ob_o),
        (hb_m, hb_o),
        (mb_m, mb_o),
        (gain_m, gain_o),
        (shift_m, shift_o),
    )
    for i, (src, dst) in enumerate(little):
        copies.append(pltpu.make_async_copy(src, dst, sem.at[len(big) + i]))
        copies[-1].start()
    for copy in copies:
        copy.wait()


def body(
    tokens,
    segment_ids,
    w_qkv,
    qv_bias,
    w_out,
    out_bias,
    w_in,
    hidden_bias,
    w_down,
    mlp_bias,
    ln_gain,
    ln_bias,
    cotangent,
    *,
    dp,
):
    seqs, length, width = tokens.shape
    count = seqs * length
    local = w_qkv.shape[2]
    hidden = w_in.shape[1]
    pairs = local // (2 * HEAD)
    stride = dp // WAYS
    strip = width // WAYS
    pieces = 2 * (hidden // TILE) + 2 + pairs
    hbm = pl.BlockSpec(memory_space=pl.ANY)
    vmem = pl.BlockSpec(memory_space=pltpu.VMEM)
    dma = pltpu.SemaphoreType.DMA
    wide = (count, width)
    big = (
        pltpu.VMEM(wide, BF),
        pltpu.VMEM(wide, BF),
        pltpu.VMEM((3, strip, local), F32),
        pltpu.VMEM((strip, local), F32),
        pltpu.VMEM((strip, hidden), F32),
        pltpu.VMEM((strip, hidden), F32),
    )
    outs = pl.pallas_call(
        functools.partial(kernel, stride),
        out_shape=big + (pltpu.VMEM((16, width), F32),),
        in_specs=[hbm, vmem, hbm, vmem, hbm, vmem, hbm, vmem, hbm, vmem, vmem, vmem, hbm],
        out_specs=(vmem,) * 7,
        scratch_shapes=[
            pltpu.VMEM(wide, BF),
            pltpu.VMEM(wide, BF),
            pltpu.VMEM((width, 3 * local), BF),
            pltpu.VMEM((2, width, local), BF),
            pltpu.VMEM((width, hidden), BF),
            pltpu.VMEM((width, hidden), BF),
            pltpu.VMEM((16, width), F32),
            pltpu.VMEM(wide, BF),
            pltpu.VMEM(wide, F32),
            pltpu.VMEM((count, 1), F32),
            pltpu.VMEM((count, 3 * local), BF),
            pltpu.VMEM((seqs * pairs, length, 2 * length), F32),
            pltpu.VMEM((2, count, local), BF),
            pltpu.VMEM(wide, F32),
            pltpu.VMEM(wide, F32),
            pltpu.VMEM((count, 1), F32),
            pltpu.VMEM(wide, BF),
            pltpu.VMEM((count, hidden), F32),
            pltpu.VMEM((count, hidden), BF),
            pltpu.VMEM((count, hidden), BF),
            pltpu.VMEM(wide, BF),
            pltpu.VMEM(wide, BF),
            pltpu.VMEM(wide, BF),
            pltpu.VMEM(wide, BF),
            pltpu.VMEM(wide, BF),
            pltpu.VMEM(wide, BF),
            pltpu.VMEM((count, local), BF),
            pltpu.VMEM((count // 2, local), BF),
            pltpu.VMEM((count // 2, width), BF),
            pltpu.VMEM((2, strip, local), BF),
            pltpu.VMEM((count, 3 * local), BF),
            pltpu.VMEM((pieces, 2, 2, 2, 2, strip, TILE), BF),
            pltpu.VMEM((pieces, 2, 2, 2, strip, TILE), BF),
            pltpu.VMEM((pieces, 2, 2, strip, TILE), BF),
            pltpu.VMEM((pieces, 2, strip, TILE), BF),
            pltpu.VMEM((pieces, strip, TILE), BF),
            pltpu.VMEM((BITS + 2, 16, width), F32),
            pltpu.VMEM((BITS + 1, 16, width), F32),
            dma((5 + 3 * pairs,)),
            dma((4, 2)),
            dma((4, 2)),
            dma((seqs, pairs)),
            dma((seqs, pairs)),
            dma((3, count // BLOCK, width // 256)),
            dma((3, count // BLOCK, width // 256)),
            dma((5,)),
            dma((5,)),
            dma((pieces, BITS)),
            dma((pieces, BITS)),
            dma((BITS + 1,)),
            dma((BITS + 1,)),
        ],
        compiler_params=pltpu.CompilerParams(
            collective_id=0, has_side_effects=True, vmem_limit_bytes=58 * 2**20
        ),
        cost_estimate=pl.CostEstimate(
            flops=12 * 10**9, bytes_accessed=12 * 10**6, transcendentals=4 * 10**6
        ),
    )(
        tokens.reshape(wide),
        segment_ids,
        w_qkv.transpose(1, 0, 2),
        qv_bias,
        w_out,
        out_bias,
        w_in,
        hidden_bias,
        w_down,
        mlp_bias,
        ln_gain,
        ln_bias,
        cotangent.reshape(wide),
    )
    if stride > 1:
        groups = [[g * stride + i for i in range(stride)] for g in range(WAYS)]
        scatter = functools.partial(
            lax.psum_scatter, axis_name="dp", axis_index_groups=groups, tiled=True
        )
        outs = (
            *outs[:2],
            scatter(outs[2], scatter_dimension=1),
            *[scatter(v, scatter_dimension=0) for v in outs[3:6]],
            lax.psum(outs[6], "dp", axis_index_groups=groups),
        )
    shapes = [
        outs[0],
        outs[1],
        outs[2],
        jax.ShapeDtypeStruct((2, local), F32),
        outs[3],
        jax.ShapeDtypeStruct((width,), F32),
        outs[4],
        jax.ShapeDtypeStruct((hidden,), F32),
        outs[5],
        jax.ShapeDtypeStruct((width,), F32),
        jax.ShapeDtypeStruct((2, width), F32),
        jax.ShapeDtypeStruct((2, width), F32),
    ]
    done = pl.pallas_call(
        deliver,
        out_shape=tuple(jax.ShapeDtypeStruct(v.shape, v.dtype) for v in shapes),
        in_specs=[vmem] * 7,
        out_specs=(hbm,) * 12,
        scratch_shapes=[pltpu.VMEM(shapes[i].shape, F32) for i in (3, 5, 7, 9, 10, 11)] + [dma((12,))],
    )(*[pltpu.with_memory_space_constraint(v, pltpu.VMEM) for v in outs])
    return (
        done[0].reshape(tokens.shape),
        done[1].reshape(tokens.shape),
        done[2].transpose(1, 0, 2),
        *done[3:],
    )


def solution(mesh):
    return jax.shard_map(
        functools.partial(body, dp=mesh.shape["dp"]),
        mesh=mesh,
        in_specs=(
            P("dp", None, None),
            P("dp", None),
            P(None, None, "tensor"),
            P(None, "tensor"),
            P(None, "tensor"),
            P(),
            P(None, "tensor"),
            P("tensor"),
            P(None, "tensor"),
            P(),
            P(),
            P(),
            P("dp", None, None),
        ),
        out_specs=(
            P("dp", None, None),
            P("dp", None, None),
            P("dp", None, "tensor"),
            P(None, "tensor"),
            P("dp", "tensor"),
            P(),
            P("dp", "tensor"),
            P("tensor"),
            P("dp", "tensor"),
            P(),
            P(),
            P(),
        ),
        check_vma=False,
    )
```

```python
import functools

import jax
import jax.numpy as jnp
from jax import lax
from jax.experimental import pallas as pl
from jax.experimental.pallas import tpu as pltpu
from jax.sharding import PartitionSpec as P

MESH = pl.DeviceIdType.MESH
BF = jnp.bfloat16
F32 = jnp.float32
HEAD = 64
NORM_EPS = 1e-06
MASKED = -1000000000.0
BITS = 4
WAYS = 2**BITS
BLOCK = 256
CHUNK = 64
TILE = 384

PLAN = (
    ("prod", 0), ("prod", 7), ("mb", 1), ("pass", 0, 0), ("prod", 4), ("pass", 7, 0), ("prod", 2),
    ("prod", 1), ("prod", 3), ("resid", 0), ("pass", 2, 0), ("pass", 3, 0), ("pass", 4, 0),
    ("pass", 1, 0), ("resid", 1), ("prod", 8), ("pass", 0, 1), ("prod", 12), ("pass", 8, 0),
    ("attb", 0, 1), ("mlp", 1), ("pass", 7, 1), ("attb", 1, 0), ("prod", 5), ("pass", 2, 1),
    ("pass", 3, 1), ("attb", 0, 0), ("attb", 0, 2), ("pass", 5, 0), ("attb", 1, 2), ("prod", 11),
    ("mixb", 0), ("pass", 1, 1), ("pass", 12, 0), ("pass", 0, 2), ("attb", 1, 1), ("mixb", 1),
    ("prod", 6), ("v", 0), ("pass", 2, 2), ("sda", 0), ("pass", 8, 1), ("pass", 3, 2),
    ("pass", 11, 0), ("prod", 9), ("prod", 10), ("pass", 5, 1), ("mlp", 0), ("pass", 6, 0),
    ("fb", 1), ("v", 1), ("v", 2), ("pass", 1, 2), ("pass", 12, 1), ("pass", 11, 1), ("sda", 1),
    ("pass", 8, 2), ("pass", 5, 2), ("pass", 9, 0), ("pass", 7, 2), ("v", 3), ("pass", 12, 2),
    ("pass", 10, 0), ("pass", 6, 1), ("pass", 11, 2), ("v", 4), ("ft", 0), ("fin", 3),
    ("pass", 4, 1), ("pass", 9, 1), ("pass", 6, 2), ("fo",), ("pass", 10, 1), ("fin", 0), ("ft", 1),
    ("pass", 4, 2), ("pass", 9, 2), ("fin", 5), ("fin", 1), ("pass", 10, 2), ("fb", 0), ("fin", 7),
    ("fin", 4), ("fin", 2), ("fin", 9), ("fin", 6), ("v", 5), ("foe",), ("fin", 11), ("fin", 10),
    ("gt", 0), ("gt", 1),
)
HALVINGS = (
    (0, 1, 2, 3),
    (0, 1, 2, 3),
    (0, 1, 2, 3),
    (0, 1, 2, 3),
    (0, 2, 1, 3),
    (0, 1, 2, 3),
    (0, 1, 2, 3),
    (0, 2, 1, 3),
    (0, 2, 1, 3),
    (0, 1, 2, 3),
    (0, 1, 2, 3),
    (0, 2, 1, 3),
    (0, 1, 2, 3),
)

NN = ((1,), (0,))
NT = ((1,), (1,))
TN = ((0,), (0,))


def dot(a, b, dims):
    return lax.dot_general(a, b, (dims, ((), ())), preferred_element_type=F32)


def each(count, step):
    for i in range(count):
        step(i)


def rows(i, size):
    if isinstance(i, int):
        return slice(i * size, (i + 1) * size)
    return pl.ds(pl.multiple_of(i * size, size), size)


cols = rows


def kernel(
    stride,
    tok_h,
    seg_ref,
    wqkv_h,
    qvb_ref,
    wout_h,
    ob_ref,
    win_h,
    hb_ref,
    wdn_h,
    mb_ref,
    gain_ref,
    shift_ref,
    dy_h,
    block_ref,
    gtok_ref,
    gqkv_ref,
    gout_ref,
    gin_ref,
    gdn_ref,
    vout,
    tok,
    dy,
    wq,
    wo,
    win,
    wdn,
    vin,
    a_buf,
    xh1,
    r1,
    qkv,
    p_buf,
    o_buf,
    h_buf,
    xh2,
    r2,
    c_buf,
    back_buf,
    g_buf,
    du_buf,
    dc_snd,
    dc_rcv,
    mlp_snd,
    mlp_rcv,
    da_snd,
    da_rcv,
    do_buf,
    do_snd,
    dhb,
    fo_buf,
    dp_buf,
    grads,
    r0_buf,
    r1_buf,
    r2_buf,
    r3_buf,
    vsum,
    vrcv,
    in_sem,
    wo_send,
    wo_recv,
    o_send,
    o_recv,
    x_send,
    x_recv,
    y_send,
    y_recv,
    g_send,
    g_recv,
    v_send,
    v_recv,
):
    d = lax.axis_index("dp")
    t = lax.axis_index("tensor")
    group = d // stride
    bit = [lax.rem(group // (2**b), 2) for b in range(BITS)]
    mate = [d + (1 - 2 * bit[b]) * (2**b) * stride for b in range(BITS)]
    count, width = tok.shape
    seqs = seg_ref.shape[0]
    length = count // seqs
    local = wo.shape[2]
    pairs = local // (2 * HEAD)
    hidden = win.shape[1]
    scale = HEAD ** (-0.5)
    vacc = vsum.at[0]

    barrier = pltpu.get_barrier_semaphore()
    for b in reversed(range(BITS)):
        pl.semaphore_signal(barrier, inc=1, device_id=(mate[b], t), device_id_type=MESH)
    pl.semaphore_signal(barrier, inc=1, device_id=(d, 1 - t), device_id_type=MESH)

    loads = []

    def load(src, dst):
        copy = pltpu.make_async_copy(src, dst, in_sem.at[len(loads)])
        copy.start()
        loads.append(copy)
        return copy

    tok_load = load(tok_h, tok)
    wq_loads = [
        load(
            wqkv_h.at[kind, :, p * 128 : (p + 1) * 128],
            wq.at[:, p * 384 + kind * 128 : p * 384 + (kind + 1) * 128],
        )
        for p in range(pairs)
        for kind in range(3)
    ]
    dy_load = load(dy_h, dy)
    wo_load = load(wout_h, wo.at[t])
    win_load = load(win_h, win)
    wdn_load = load(wdn_h, wdn)

    def across(src, dst, send, recv):
        return pltpu.make_async_remote_copy(
            src_ref=src,
            dst_ref=dst,
            send_sem=send,
            recv_sem=recv,
            device_id=(d, 1 - t),
            device_id_type=MESH,
        )

    def toward(b, src, dst, send, recv):
        return pltpu.make_async_remote_copy(
            src_ref=src,
            dst_ref=dst,
            send_sem=send,
            recv_sem=recv,
            device_id=(mate[b], t),
            device_id_type=MESH,
        )

    slab = width // 8

    def wo_rows(turned, part):
        first = bit[0]
        second = 1 - bit[1] if turned else bit[1]
        return rows((2 * second + first) * 2 + part, slab)

    def wo_copy(step, part):
        sems = wo_send.at[step, part], wo_recv.at[step, part]
        if step == 0:
            here = wo_rows(False, part)
            return across(wout_h.at[here], wo.at[t, here], *sems)
        here = wo_rows(step == 3, part)
        return toward(1 if step == 2 else 0, wo.at[1 - t, here], wo.at[1 - t, here], *sems)

    def wo_share(part):
        wo_copy(0, part).wait_recv()
        wo_copy(2, part).start()
        wo_copy(1, part).start()

    def wo_forward(part):
        wo_copy(2, part).wait_recv()
        wo_copy(3, part).start()

    def o_copy(s, p):
        here = rows(s, length)
        place = o_buf.at[t, here, cols(p, 128)]
        return across(place, place, o_send.at[s, p], o_recv.at[s, p])

    half = length // 2

    def mine(s):
        return rows(2 * s + t, half)

    def theirs(s):
        return rows(2 * s + 1 - t, half)

    def dc_copy(n, i):
        here = theirs(n), cols(i, 256)
        return across(
            dc_snd.at[here], dc_rcv.at[here], x_send.at[0, n, i], x_recv.at[0, n, i]
        )

    def da_copy(s, i):
        here = theirs(s), cols(i, 256)
        return across(
            da_snd.at[here], da_rcv.at[here], x_send.at[1, s, i], x_recv.at[1, s, i]
        )

    def mlp_copy(s, i):
        here = rows(s, length), cols(i, 256)
        return across(
            mlp_snd.at[here], mlp_rcv.at[here], x_send.at[2, s, i], x_recv.at[2, s, i]
        )

    def do_copy(s):
        return across(do_snd.at[rows(s, half)], do_buf.at[mine(s)], y_send.at[s], y_recv.at[s])

    def gt_copy(s):
        here = gtok_ref.at[mine(s)]
        return across(here, here, y_send.at[2 + s], y_recv.at[2 + s])

    def fo_copy():
        return across(fo_buf.at[0], fo_buf.at[1], y_send.at[4], y_recv.at[4])

    wide = width // 256

    vacc[...] = jnp.zeros(vacc.shape, F32)
    vin[0:2] = gain_ref[...].astype(F32)
    vin[2:4] = shift_ref[...].astype(F32)
    vin[4:5] = ob_ref[...].astype(F32).reshape(1, width)
    vin[5:6] = mb_ref[...].astype(F32).reshape(1, width)
    line = hb_ref[...].astype(F32).reshape(1, hidden)
    vin[6:7] = line[:, :width]
    vin[7:8] = line[:, width:]
    vin[8:9, :local] = qvb_ref[0:1].astype(F32)
    vin[8:9, local:] = qvb_ref[1:2].astype(F32)

    lane = lax.broadcasted_iota(jnp.int32, (1, 128), 1)
    low_half = lane < HEAD

    def stacked(value):
        zero = jnp.zeros_like(value)
        return jnp.concatenate(
            [jnp.where(low_half, value, zero), jnp.where(low_half, zero, value)], axis=0
        )

    def normalize(value):
        mean = jnp.sum(value, axis=-1, keepdims=True) * (1.0 / width)
        center = value - mean
        spread = jnp.sum(center * center, axis=-1, keepdims=True) * (1.0 / width)
        scale_back = lax.rsqrt(spread + NORM_EPS)
        return center * scale_back, scale_back

    def norm_back(grad, normed, scale_back, gain):
        inner = grad * gain
        mean_one = jnp.sum(inner, axis=-1, keepdims=True) * (1.0 / width)
        mean_two = jnp.sum(inner * normed, axis=-1, keepdims=True) * (1.0 / width)
        return scale_back * (inner - mean_one - normed * mean_two)

    def same_image(s):
        ids = seg_ref[s : s + 1].astype(F32)
        down = jnp.broadcast_to(ids, (128, length)).T
        return jnp.concatenate(
            [down == ids[:, i * 128 : (i + 1) * 128] for i in range(length // 128)], axis=1
        )

    def norm_one(s):
        def step(i):
            here = rows(s * (length // CHUNK) + i, CHUNK)
            normed, scale_back = normalize(tok[here].astype(F32))
            xh1[here] = normed
            r1[here] = scale_back
            a_buf[here] = (normed * vin[0:1] + vin[2:3]).astype(BF)

        each(length // CHUNK, step)

    def attention(s, after):
        seq = rows(s, length)
        allowed = same_image(s)

        def pair_step(p):
            bias = jnp.concatenate(
                [
                    vin[8:9, cols(p, 128)],
                    jnp.zeros((1, 128), F32),
                    vin[8:9, cols(pairs + p, 128)],
                ],
                axis=1,
            )
            mixed = (dot(a_buf[seq], wq[:, cols(p, 384)], NN) + bias).astype(BF)
            qkv[seq, cols(p, 384)] = mixed
            scores = dot(mixed[:, :128], stacked(mixed[:, 128:256]), NT) * scale
            soft = []
            for e in range(2):
                one = jnp.where(allowed, scores[:, e * length : (e + 1) * length], MASKED)
                expo = jnp.exp(one - jnp.max(one, axis=-1, keepdims=True))
                soft.append(expo * (1.0 / jnp.sum(expo, axis=-1, keepdims=True)))
            both = jnp.concatenate(soft, axis=1)
            p_buf[s * pairs + p] = both
            o_buf[t, seq, cols(p, 128)] = dot(
                both.astype(BF), stacked(mixed[:, 256:]), NN
            ).astype(BF)
            o_copy(s, p).start()
            after(p)

        each(pairs, pair_step)

    tok_load.wait()
    norm_one(0)
    norm_one(1)
    pl.semaphore_wait(barrier, BITS + 1)
    wo_copy(0, 0).start()
    wo_copy(0, 1).start()
    for copy in wq_loads:
        copy.wait()
    attention(0, lambda p: None)

    def bring(p):
        if p > 0:
            wo_share(p - 1)

    attention(1, bring)

    strip = width // WAYS
    received = [r0_buf, r1_buf, r2_buf, r3_buf]

    def product(piece, left, right, order):
        full = dot(left, right, TN)
        for k in range(WAYS):
            b = [(k >> i) & 1 for i in order]
            grads[piece, b[0], b[1], b[2], b[3]] = full[k * strip : (k + 1) * strip].astype(BF)
        g_copy(piece, 0, order).start()

    def own(piece, depth, order):
        return (piece,) + tuple(bit[b] for b in order[:depth])

    def g_copy(piece, k, order):
        return toward(
            order[k],
            grads.at[own(piece, k, order) + (1 - bit[order[k]],)],
            received[k].at[piece],
            g_send.at[piece, k],
            g_recv.at[piece, k],
        )

    def pass_on(piece, k, order):
        g_copy(piece, k, order).wait_recv()
        here = own(piece, k + 1, order)
        grads[here] = (grads[here].astype(F32) + received[k][piece].astype(F32)).astype(BF)
        g_copy(piece, k + 1, order).start()

    def finish(piece, order):
        g_copy(piece, 3, order).wait_recv()
        return grads[own(piece, 4, order)].astype(F32) + received[3][piece].astype(F32)

    hidden_pieces = hidden // TILE
    down, into, outs, mixes = 0, hidden_pieces, 2 * hidden_pieces, 2 * hidden_pieces + 1
    others = mixes + pairs
    total = others + 1

    dy_load.wait()
    vacc[3:4] += jnp.sum(dy[...].astype(F32), axis=0, keepdims=True)
    wdn_load.wait()

    def hidden_back(i):
        back_buf[:, cols(i, 256)] = dot(dy[...], wdn[:, cols(i, 256)], NN)

    each(hidden // 256, hidden_back)
    wo_load.wait()
    win_load.wait()
    for part in range(2):
        wo_forward(part)
    for part in range(2):
        wo_copy(1, part).wait_recv()
        wo_copy(3, part).wait_recv()

    def middle(n):
        here = rows(n, BLOCK)

        for p in range(pairs):
            o_copy(n, p).wait_recv()

        h_buf[here] = dot(o_buf[0, here], wo[0], NT) + dot(o_buf[1, here], wo[1], NT)

        def norm_step(i):
            few = rows(n * (BLOCK // CHUNK) + i, CHUNK)
            resid = h_buf[few] + vin[4:5] + tok[few].astype(F32)
            h_buf[few] = resid
            normed, scale_back = normalize(resid)
            xh2[few] = normed
            r2[few] = scale_back
            c_buf[few] = (normed * vin[1:2] + vin[3:4]).astype(BF)

        each(BLOCK // CHUNK, norm_step)

        for m in range(hidden // width):

            def hidden_step(i, m=m):
                there = cols(i, 256)
                part = cols(m * wide + i, 256)
                pre = dot(c_buf[here], win[:, part], NN) + vin[6 + m : 7 + m, there]
                phi = 0.5 + 0.5 * lax.erf(pre * 0.7071067811865476)
                g_buf[here, part] = (pre * phi).astype(BF)
                slope = phi + pre * (jnp.exp(-0.5 * pre * pre) * 0.3989422804014327)
                low = (back_buf[here, part] * slope).astype(BF)
                du_buf[here, part] = low
                vacc[1 + m : 2 + m, there] += jnp.sum(low.astype(F32), axis=0, keepdims=True)

            each(wide, hidden_step)

    def normed_back(n):
        here = rows(n, BLOCK)

        def back_step(i):
            there = cols(i, 256)
            grad = dot(du_buf[here], win[rows(i, 256)], NT)
            dc_snd[here, there] = grad.astype(BF)
            dc_copy(n, i).start()
            vacc[10:11, there] += jnp.sum(grad * xh2[here, there], axis=0, keepdims=True)
            vacc[12:13, there] += jnp.sum(grad, axis=0, keepdims=True)

        each(wide, back_step)

    middle(0)
    normed_back(0)
    middle(1)

    def mlp_out(s):
        seq = rows(s, length)

        def step(i):
            mlp_snd[seq, cols(i, 256)] = dot(g_buf[seq], wdn[rows(i, 256)], NT).astype(BF)
            mlp_copy(s, i).start()

        each(wide, step)

    def resid_back(s):
        for i in range(wide):
            dc_copy(s, i).wait_recv()

        def step(i):
            here = rows((2 * s + t) * (half // CHUNK) + i, CHUNK)
            grad = dc_snd[here].astype(F32) + dc_rcv[here].astype(F32)
            full = dy[here].astype(F32) + norm_back(grad, xh2[here], r2[here], vin[1:2])
            xh2[here] = full
            dhb[rows(s * (half // CHUNK) + i, CHUNK)] = full.astype(BF)
            vacc[8:9] += jnp.sum(full, axis=0, keepdims=True)

        each(half // CHUNK, step)
        low = dhb[rows(s, half)]
        do_snd[rows(s, half)] = dot(low, wo[1 - t], NN).astype(BF)
        do_copy(s).start()
        do_buf[mine(s)] = dot(low, wo[t], NN).astype(BF)

    def attention_back(s, p):
        seq = rows(s, length)
        if (s, p) in heads_first:
            do_copy(s).wait_recv()
        mixed = qkv[seq, cols(p, 384)]
        query, keys = mixed[:, :128], stacked(mixed[:, 128:256])
        grad_o = do_buf[seq, cols(p, 128)]
        soft = p_buf[s * pairs + p]
        grad_soft = dot(grad_o, stacked(mixed[:, 256:]), NT)
        parts = []
        for e in range(2):
            one, two = (v[:, e * length : (e + 1) * length] for v in (soft, grad_soft))
            delta = jnp.sum(one * two, axis=-1, keepdims=True)
            parts.append((one * (two - delta)).astype(BF))
        grad_scores = jnp.concatenate(parts, axis=1)
        grad_query = dot(grad_scores, keys, NN) * scale
        grad_keys = dot(grad_scores, query, TN) * scale
        grad_keys = jnp.where(low_half, grad_keys[:length], grad_keys[length:])
        grad_values = dot(soft.astype(BF), grad_o, TN)
        grad_values = jnp.where(low_half, grad_values[:length], grad_values[length:])
        low = [v.astype(BF) for v in (grad_query, grad_keys, grad_values)]
        dp_buf[seq, cols(p, 384)] = jnp.concatenate(low, axis=1)
        vacc[0:1, cols(p, 128)] += jnp.sum(low[0].astype(F32), axis=0, keepdims=True)
        vacc[0:1, cols(pairs + p, 128)] += jnp.sum(low[2].astype(F32), axis=0, keepdims=True)

    def mixed_back(s):
        seq = rows(s, length)

        def step(i):
            here = cols(i, 256)
            grad = dot(dp_buf[seq], wq[rows(i, 256)], NT)
            da_snd[seq, here] = grad.astype(BF)
            vacc[9:10, here] += jnp.sum(grad * xh1[seq, here], axis=0, keepdims=True)
            vacc[11:12, here] += jnp.sum(grad, axis=0, keepdims=True)

        each(wide, step)

    def send_mixed(s):
        for i in range(wide):
            da_copy(s, i).start()

    def finish_block(s):
        seq = rows(s, length)

        def step(i):
            mlp_copy(s, i).wait_recv()
            here = seq, cols(i, 256)
            added = mlp_snd[here].astype(F32) + mlp_rcv[here].astype(F32)
            block_ref[seq, cols(i, 256)] = (h_buf[here] + (added + vin[5:6, cols(i, 256)])).astype(BF)

        each(wide, step)

    def finish_tokens(s):
        for i in range(wide):
            da_copy(s, i).wait_recv()

        def step(i):
            here = rows((2 * s + t) * (half // CHUNK) + i, CHUNK)
            grad = da_snd[here].astype(F32) + da_rcv[here].astype(F32)
            full = xh2[here] + norm_back(grad, xh1[here], r1[here], vin[0:1])
            gtok_ref[here] = full.astype(BF)

        each(half // CHUNK, step)
        gt_copy(s).start()

    def v_copy(k):
        sems = v_send.at[k], v_recv.at[k]
        if k == 0:
            shared = pl.ds(8, 8)
            return across(vsum.at[0, shared], vrcv.at[0, shared], *sems)
        return toward(k - 1, vsum.at[k], vrcv.at[k], *sems)

    def v_next(k):
        v_copy(k).wait_recv()
        if k == 0:
            vsum[1, :8] = vsum[0, :8]
            vsum[1, 8:] = vsum[0, 8:] + vrcv[0, 8:]
        else:
            vsum[k + 1] = vsum[k] + vrcv[k]
        if k < BITS:
            v_copy(k + 1).start()

    def prod(piece):
        order = HALVINGS[piece]
        if piece < into:
            product(piece, dy[...], g_buf[:, cols(piece, TILE)], order)
        elif piece < outs:
            product(piece, c_buf[...], du_buf[:, cols(piece - into, TILE)], order)
        elif piece in (outs, others):
            side = t if piece == outs else 1 - t
            heads = jnp.concatenate([o_buf[side, mine(s)] for s in range(seqs)], axis=0)
            product(piece, dhb[...], heads, order)
        else:
            product(piece, a_buf[...], dp_buf[:, cols(piece - mixes, 384)], order)

    def fin(piece):
        value = finish(piece, HALVINGS[piece])
        if piece < into:
            gdn_ref[:, cols(piece, TILE)] = value
        elif piece < outs:
            gin_ref[:, cols(piece - into, TILE)] = value
        else:
            for kind in range(3):
                gqkv_ref[kind, :, cols(piece - mixes, 128)] = value[:, cols(kind, 128)]

    def outer_send():
        fo_buf[0] = finish(others, HALVINGS[others]).astype(BF)
        fo_copy().start()

    def outer_end():
        value = finish(outs, HALVINGS[outs])
        fo_copy().wait_recv()
        gout_ref[...] = value + fo_buf[1].astype(F32)

    heads_first = {}
    for name, *which in PLAN:
        if name == "attb":
            heads_first.setdefault(which[0], tuple(which))
    heads_first = tuple(heads_first.values())

    def small(k):
        if k == 0:
            v_copy(0).start()
        else:
            v_next(k - 1)
        if k == BITS + 1:
            vout[...] = vsum[k]

    steps = {
        "prod": prod,
        "pass": lambda piece, k: pass_on(piece, k, HALVINGS[piece]),
        "fin": fin,
        "mb": normed_back,
        "resid": resid_back,
        "attb": attention_back,
        "mixb": mixed_back,
        "sda": send_mixed,
        "mlp": mlp_out,
        "fb": finish_block,
        "ft": finish_tokens,
        "gt": lambda s: gt_copy(s).wait_recv(),
        "fo": outer_send,
        "foe": outer_end,
        "v": small,
    }
    for name, *which in PLAN:
        steps[name](*which)

    for part in range(2):
        for step in range(4):
            wo_copy(step, part).wait_send()
    for s in range(seqs):
        for p in range(pairs):
            o_copy(s, p).wait_send()
        for i in range(wide):
            da_copy(s, i).wait_send()
            mlp_copy(s, i).wait_send()
            dc_copy(s, i).wait_send()
        do_copy(s).wait_send()
        gt_copy(s).wait_send()
    fo_copy().wait_send()
    for piece in range(total):
        for k in range(BITS):
            g_copy(piece, k, HALVINGS[piece]).wait_send()
    for k in range(BITS + 1):
        v_copy(k).wait_send()


def deliver(
    block_v,
    gtok_v,
    gqkv_v,
    gout_v,
    gin_v,
    gdn_v,
    small,
    block_o,
    gtok_o,
    gqkv_o,
    pair_o,
    gout_o,
    ob_o,
    gin_o,
    hb_o,
    gdn_o,
    mb_o,
    gain_o,
    shift_o,
    pair_m,
    ob_m,
    hb_m,
    mb_m,
    gain_m,
    shift_m,
    sem,
):
    big = (
        (block_v, block_o),
        (gtok_v, gtok_o),
        (gqkv_v, gqkv_o),
        (gout_v, gout_o),
        (gin_v, gin_o),
        (gdn_v, gdn_o),
    )
    copies = [pltpu.make_async_copy(src, dst, sem.at[i]) for i, (src, dst) in enumerate(big)]
    for copy in copies:
        copy.start()
    local, width, hidden = pair_o.shape[1], ob_o.shape[0], hb_o.shape[0]
    pair_m[0:1] = small[0:1, :local]
    pair_m[1:2] = small[0:1, local:]
    hb_m[...] = jnp.concatenate([small[1:2], small[2:3]], axis=1).reshape(hidden)
    ob_m[...] = small[8:9].reshape(width)
    mb_m[...] = small[3:4].reshape(width)
    gain_m[...] = small[9:11]
    shift_m[...] = small[11:13]
    little = (
        (pair_m, pair_o),
        (ob_m, ob_o),
        (hb_m, hb_o),
        (mb_m, mb_o),
        (gain_m, gain_o),
        (shift_m, shift_o),
    )
    for i, (src, dst) in enumerate(little):
        copies.append(pltpu.make_async_copy(src, dst, sem.at[len(big) + i]))
        copies[-1].start()
    for copy in copies:
        copy.wait()


def body(
    tokens,
    segment_ids,
    w_qkv,
    qv_bias,
    w_out,
    out_bias,
    w_in,
    hidden_bias,
    w_down,
    mlp_bias,
    ln_gain,
    ln_bias,
    cotangent,
    *,
    dp,
):
    seqs, length, width = tokens.shape
    count = seqs * length
    local = w_qkv.shape[2]
    hidden = w_in.shape[1]
    pairs = local // (2 * HEAD)
    stride = dp // WAYS
    strip = width // WAYS
    pieces = 2 * (hidden // TILE) + 2 + pairs
    hbm = pl.BlockSpec(memory_space=pl.ANY)
    vmem = pl.BlockSpec(memory_space=pltpu.VMEM)
    dma = pltpu.SemaphoreType.DMA
    wide = (count, width)
    big = (
        pltpu.VMEM(wide, BF),
        pltpu.VMEM(wide, BF),
        pltpu.VMEM((3, strip, local), F32),
        pltpu.VMEM((strip, local), F32),
        pltpu.VMEM((strip, hidden), F32),
        pltpu.VMEM((strip, hidden), F32),
    )
    outs = pl.pallas_call(
        functools.partial(kernel, stride),
        out_shape=big + (pltpu.VMEM((16, width), F32),),
        in_specs=[hbm, vmem, hbm, vmem, hbm, vmem, hbm, vmem, hbm, vmem, vmem, vmem, hbm],
        out_specs=(vmem,) * 7,
        scratch_shapes=[
            pltpu.VMEM(wide, BF),
            pltpu.VMEM(wide, BF),
            pltpu.VMEM((width, 3 * local), BF),
            pltpu.VMEM((2, width, local), BF),
            pltpu.VMEM((width, hidden), BF),
            pltpu.VMEM((width, hidden), BF),
            pltpu.VMEM((16, width), F32),
            pltpu.VMEM(wide, BF),
            pltpu.VMEM(wide, F32),
            pltpu.VMEM((count, 1), F32),
            pltpu.VMEM((count, 3 * local), BF),
            pltpu.VMEM((seqs * pairs, length, 2 * length), F32),
            pltpu.VMEM((2, count, local), BF),
            pltpu.VMEM(wide, F32),
            pltpu.VMEM(wide, F32),
            pltpu.VMEM((count, 1), F32),
            pltpu.VMEM(wide, BF),
            pltpu.VMEM((count, hidden), F32),
            pltpu.VMEM((count, hidden), BF),
            pltpu.VMEM((count, hidden), BF),
            pltpu.VMEM(wide, BF),
            pltpu.VMEM(wide, BF),
            pltpu.VMEM(wide, BF),
            pltpu.VMEM(wide, BF),
            pltpu.VMEM(wide, BF),
            pltpu.VMEM(wide, BF),
            pltpu.VMEM((count, local), BF),
            pltpu.VMEM((count // 2, local), BF),
            pltpu.VMEM((count // 2, width), BF),
            pltpu.VMEM((2, strip, local), BF),
            pltpu.VMEM((count, 3 * local), BF),
            pltpu.VMEM((pieces, 2, 2, 2, 2, strip, TILE), BF),
            pltpu.VMEM((pieces, 2, 2, 2, strip, TILE), BF),
            pltpu.VMEM((pieces, 2, 2, strip, TILE), BF),
            pltpu.VMEM((pieces, 2, strip, TILE), BF),
            pltpu.VMEM((pieces, strip, TILE), BF),
            pltpu.VMEM((BITS + 2, 16, width), F32),
            pltpu.VMEM((BITS + 1, 16, width), F32),
            dma((5 + 3 * pairs,)),
            dma((4, 2)),
            dma((4, 2)),
            dma((seqs, pairs)),
            dma((seqs, pairs)),
            dma((3, count // BLOCK, width // 256)),
            dma((3, count // BLOCK, width // 256)),
            dma((5,)),
            dma((5,)),
            dma((pieces, BITS)),
            dma((pieces, BITS)),
            dma((BITS + 1,)),
            dma((BITS + 1,)),
        ],
        compiler_params=pltpu.CompilerParams(
            collective_id=0, has_side_effects=True, vmem_limit_bytes=58 * 2**20
        ),
        cost_estimate=pl.CostEstimate(
            flops=12 * 10**9, bytes_accessed=12 * 10**6, transcendentals=4 * 10**6
        ),
    )(
        tokens.reshape(wide),
        segment_ids,
        w_qkv.transpose(1, 0, 2),
        qv_bias,
        w_out,
        out_bias,
        w_in,
        hidden_bias,
        w_down,
        mlp_bias,
        ln_gain,
        ln_bias,
        cotangent.reshape(wide),
    )
    if stride > 1:
        groups = [[g * stride + i for i in range(stride)] for g in range(WAYS)]
        scatter = functools.partial(
            lax.psum_scatter, axis_name="dp", axis_index_groups=groups, tiled=True
        )
        outs = (
            *outs[:2],
            scatter(outs[2], scatter_dimension=1),
            *[scatter(v, scatter_dimension=0) for v in outs[3:6]],
            lax.psum(outs[6], "dp", axis_index_groups=groups),
        )
    shapes = [
        outs[0],
        outs[1],
        outs[2],
        jax.ShapeDtypeStruct((2, local), F32),
        outs[3],
        jax.ShapeDtypeStruct((width,), F32),
        outs[4],
        jax.ShapeDtypeStruct((hidden,), F32),
        outs[5],
        jax.ShapeDtypeStruct((width,), F32),
        jax.ShapeDtypeStruct((2, width), F32),
        jax.ShapeDtypeStruct((2, width), F32),
    ]
    done = pl.pallas_call(
        deliver,
        out_shape=tuple(jax.ShapeDtypeStruct(v.shape, v.dtype) for v in shapes),
        in_specs=[vmem] * 7,
        out_specs=(hbm,) * 12,
        scratch_shapes=[pltpu.VMEM(shapes[i].shape, F32) for i in (3, 5, 7, 9, 10, 11)] + [dma((12,))],
    )(*[pltpu.with_memory_space_constraint(v, pltpu.VMEM) for v in outs])
    return (
        done[0].reshape(tokens.shape),
        done[1].reshape(tokens.shape),
        done[2].transpose(1, 0, 2),
        *done[3:],
    )


def solution(mesh):
    return jax.shard_map(
        functools.partial(body, dp=mesh.shape["dp"]),
        mesh=mesh,
        in_specs=(
            P("dp", None, None),
            P("dp", None),
            P(None, None, "tensor"),
            P(None, "tensor"),
            P(None, "tensor"),
            P(),
            P(None, "tensor"),
            P("tensor"),
            P(None, "tensor"),
            P(),
            P(),
            P(),
            P("dp", None, None),
        ),
        out_specs=(
            P("dp", None, None),
            P("dp", None, None),
            P("dp", None, "tensor"),
            P(None, "tensor"),
            P("dp", "tensor"),
            P(),
            P("dp", "tensor"),
            P("tensor"),
            P("dp", "tensor"),
            P(),
            P(),
            P(),
        ),
        check_vma=False,
    )
```
